128 devices in a mesh: shot: 8 (over x, z_lo), dom: 16 (over z_hi, y, core).
Axes of the slice: x: 4, y: 4, z: 4 (z_hi: 2, z_lo: 2; z = z_hi * 2 + z_lo), core: 2. Of those that a mesh axis runs over, the one named last changes fastest.
Arguments:
- velocity: float32 [16, 16, 4, 64, 512], P('shot', 'dom'), may hold values from 0.05 to 0.18
- fwd_prev: float32 [8, 64, 64, 512], P('shot', 'dom'), may hold values from -3 to 3
- fwd_cur: float32 [8, 64, 64, 512], P('shot', 'dom'), may hold values from -3 to 3
- adj_prev: float32 [8, 64, 64, 512], P('shot', 'dom'), may hold values from -3 to 3
- adj_cur: float32 [8, 64, 64, 512], P('shot', 'dom'), may hold values from -3 to 3
- wavelet: float32 [8, 8], P('shot'), may hold values from -24 to 24
- src_pos: int32 [8], P('shot'), may hold values from 0 to 2097151
- rec_pos: int32 [8, 256], P('shot'), may hold values from 0 to 2097151
- observed: float32 [8, 8, 256], P('shot'), may hold values from -6 to 6
- step_count: int32 [8], P('shot'), may hold values from 4 to 8
- aperture: int32 [8, 16], replicated, may hold values from 0 to 255, as said below
- block_slot: int32 [16], replicated, may hold values from 0 to 15, each once
- prev_batch: float32 [16, 16, 4, 64, 512], P('shot', 'dom'), may hold values from -6 to 6
- snapshot: float32 [16, 16, 4, 64, 512], P('shot', 'dom'), may hold values from -6 to 6
Outputs:
- reduced_grad: float32 [16, 16, 4, 64, 512], P('shot', 'dom')
The draws below stay inside these ranges and needn't reach their ends.
Inputs may be any that keep to these rules, and one draw needn't show every extreme that they name: `aperture`: row s is (b0 + k) * 8 + y for k = 0 .. 15, with b0 in 0 .. 16 and y in 0 .. 7 taken per row.
All inputs are finite; a program needn't handle non-finite values.
Results may differ from the reference program's by a relative error of at most 0.0003.
Values sent between devices are 32-bit elements; how exact they have to be, the bound alone decides.
A program may use at most 128 MiB of HBM per device.

```python
import math
import jax
import jax.numpy as jnp
from jax import lax

CX = 4
AY = 64
NZ = 512
NREC = 256
STEPS = 8
SHOTS = 8
SLOTS = 16
NBY = 8
NBLK = 256
AX = 64
N_DOM = 16


def draw_step_count(key, part):
    key = jax.random.fold_in(key, 13)
    first_key, order_key = jax.random.split(key)
    counts = jax.random.randint(first_key, (SHOTS,), STEPS // 2, STEPS + 1)
    order = jax.random.permutation(order_key, SHOTS)
    counts = counts.at[order[0]].set(STEPS)
    counts = counts.at[order[1]].set(STEPS // 2)
    return counts.astype(jnp.int32)


def draw_aperture(key, part):
    key = jax.random.fold_in(key, 11)
    start_key, row_key, order_key = jax.random.split(key, 3)
    span = NBLK // (2 * NBY)
    starts = jax.random.randint(start_key, (SHOTS,), 0, span + 1)
    rows = jax.random.randint(row_key, (SHOTS,), 0, NBY)
    order = jax.random.permutation(order_key, SHOTS)
    starts = starts.at[order[0]].set(span)
    rows = rows.at[order[0]].set(NBY - 1)
    starts = starts.at[order[1]].set(0)
    rows = rows.at[order[1]].set(0)
    starts = starts.at[order[2]].set(span // 2)
    starts = starts.at[order[3]].set(1)
    ids = (starts[:, None] + jnp.arange(span)[None, :]) * NBY + rows[:, None]
    return ids.astype(jnp.int32)


def place_ends(entries, stream_key, least, largest):
    longest = entries.shape.index(max(entries.shape))
    spots = []
    for shift in (0, 1):
        where = [jax.random.randint(jax.random.fold_in(stream_key, axis), (), 0, length) for axis, length in enumerate(entries.shape)]
        where[longest] = (where[longest] + shift) % entries.shape[longest]
        spots.append(tuple(where))
    return entries.at[spots[0]].set(least).at[spots[1]].set(largest)


def block_scale(stream_key, extent, cuts, least, largest):
    def one(dim, blocks):
        draws = jax.random.uniform(jax.random.fold_in(jax.random.fold_in(stream_key, 6), dim), (blocks,), jnp.float32, least / len(cuts), largest / len(cuts))
        return jnp.repeat(jnp.exp(draws), extent[dim] // blocks).reshape((-1,) + (1,) * (len(extent) - dim - 1))

    loudness = one(*cuts[0])
    for cut in cuts[1:]:
        loudness = loudness * one(*cut)
    return loudness


def bell_draw(own_key, shape, deviation, most, cuts=(), held_as=jnp.bfloat16):
    entries = deviation * jax.random.normal(own_key, shape, jnp.float32)
    if cuts:
        entries = entries * block_scale(own_key, shape, cuts, -0.22, 0.18)
    return jnp.clip(entries, -most, most).astype(held_as)


def setup_inputs(seed: int = 0) -> dict:
    arg_keys = jax.random.split(jax.random.key(seed), 15)
    velocity = jnp.clip(jnp.exp(math.log(0.18) - 1.2809339 * jax.random.uniform(arg_keys[0], (SLOTS, N_DOM, CX, AY, NZ), jnp.float32) ** block_scale(arg_keys[0], (SLOTS, N_DOM, CX, AY, NZ), ((0, 8), (1, 16)), -0.2, 0.2)), 0.05, 0.18)
    fwd_prev = bell_draw(arg_keys[1], (SHOTS, AX, AY, NZ), 0.3, 3.0, ((0, 8), (1, 16)), jnp.float32)
    fwd_cur = bell_draw(arg_keys[2], (SHOTS, AX, AY, NZ), 0.3, 3.0, ((0, 8), (1, 16)), jnp.float32)
    adj_prev = bell_draw(arg_keys[3], (SHOTS, AX, AY, NZ), 0.3, 3.0, ((0, 8), (1, 16)), jnp.float32)
    adj_cur = bell_draw(arg_keys[4], (SHOTS, AX, AY, NZ), 0.3, 3.0, ((0, 8), (1, 16)), jnp.float32)
    wavelet = bell_draw(arg_keys[5], (SHOTS, STEPS), 4.0, 24.0, ((0, 8),), jnp.float32)
    src_pos = place_ends(jax.random.randint(arg_keys[6], (SHOTS,), 0, AX * AY * NZ), jax.random.fold_in(arg_keys[6], 1), 0, (AX * AY * NZ) - 1).astype(jnp.int32)
    rec_pos = place_ends(jax.random.randint(arg_keys[7], (SHOTS, NREC), 0, AX * AY * NZ), jax.random.fold_in(arg_keys[7], 1), 0, (AX * AY * NZ) - 1).astype(jnp.int32)
    observed = bell_draw(arg_keys[8], (SHOTS, STEPS, NREC), 1.0, 6.0, ((0, 8),), jnp.float32)
    step_count = draw_step_count(jax.random.fold_in(arg_keys[14], 71), 0)
    aperture = draw_aperture(jax.random.fold_in(arg_keys[14], 71), 0)
    block_slot = jax.random.permutation(arg_keys[11], SLOTS).astype(jnp.int32)
    prev_batch = bell_draw(arg_keys[12], (SLOTS, N_DOM, CX, AY, NZ), 1.0, 6.0, ((0, 8), (1, 16)), jnp.float32)
    snapshot = bell_draw(arg_keys[13], (SLOTS, N_DOM, CX, AY, NZ), 1.0, 6.0, ((0, 8), (1, 16)), jnp.float32)
    return dict(velocity=velocity, fwd_prev=fwd_prev, fwd_cur=fwd_cur, adj_prev=adj_prev, adj_cur=adj_cur, wavelet=wavelet, src_pos=src_pos, rec_pos=rec_pos, observed=observed, step_count=step_count, aperture=aperture, block_slot=block_slot, prev_batch=prev_batch, snapshot=snapshot)


COEFS = (-205.0 / 72.0, 8.0 / 5.0, -1.0 / 5.0, 8.0 / 315.0, -1.0 / 560.0)


def stencil(padded):
    size_x = padded.shape[0] - 8
    size_y = padded.shape[1] - 8
    size_z = padded.shape[2] - 8
    center = padded[4:4 + size_x, 4:4 + size_y, 4:4 + size_z]
    total = (3.0 * COEFS[0]) * center
    for reach in range(1, 5):
        along_x = padded[4 + reach:4 + reach + size_x, 4:4 + size_y, 4:4 + size_z] + padded[4 - reach:4 - reach + size_x, 4:4 + size_y, 4:4 + size_z]
        along_y = padded[4:4 + size_x, 4 + reach:4 + reach + size_y, 4:4 + size_z] + padded[4:4 + size_x, 4 - reach:4 - reach + size_y, 4:4 + size_z]
        along_z = padded[4:4 + size_x, 4:4 + size_y, 4 + reach:4 + reach + size_z] + padded[4:4 + size_x, 4:4 + size_y, 4 - reach:4 - reach + size_z]
        total = total + COEFS[reach] * (along_x + along_y + along_z)
    return total


def laplacian(field):
    return stencil(jnp.pad(field, 4))


def reference(velocity, fwd_prev, fwd_cur, adj_prev, adj_cur, wavelet, src_pos, rec_pos, observed, step_count, aperture, block_slot, prev_batch, snapshot):
    slab_shape = (N_DOM * CX, AY, NZ)

    def run_shot(total, inputs):
        blocks, u_prev, u_cur, p_prev, p_cur, wave, source, receivers, recorded, count = inputs
        block_x = blocks // NBY
        block_y = blocks % NBY
        slots = block_slot[(block_x // N_DOM) * NBY + block_y].astype(jnp.int32)
        cols = (block_x % N_DOM).astype(jnp.int32)
        model = velocity[slots, cols].reshape(slab_shape)
        laps = []
        samples = []
        for step in range(STEPS):
            active = step < count
            lap = laplacian(u_cur)
            u_next = 2.0 * u_cur - u_prev + model * lap
            u_next = u_next.reshape(-1).at[source].add(wave[step]).reshape(slab_shape)
            u_prev, u_cur = jnp.where(active, u_cur, u_prev), jnp.where(active, u_next, u_cur)
            laps.append(lap)
            samples.append(u_cur.reshape(-1)[receivers])
        grad = jnp.zeros(slab_shape, jnp.float32)
        for step in reversed(range(STEPS)):
            active = step < count
            residual = jnp.where(active, samples[step] - recorded[step], 0.0)
            p_hit = p_cur.reshape(-1).at[receivers].add(residual).reshape(slab_shape)
            grad = grad + jnp.where(active, p_hit * laps[step], 0.0)
            p_next = 2.0 * p_hit - p_prev + laplacian(model * p_hit)
            p_prev, p_cur = jnp.where(active, p_hit, p_prev), jnp.where(active, p_next, p_cur)
        total = total.at[slots, cols].add(grad.reshape((N_DOM, CX, AY, NZ)))
        return total, None

    start = jnp.zeros(velocity.shape, jnp.float32)
    batch, _ = lax.scan(run_shot, start, (aperture, fwd_prev, fwd_cur, adj_prev, adj_cur, wavelet, src_pos, rec_pos, observed, step_count))
    return (batch - prev_batch) + snapshot
```

```python
import functools

import jax
import jax.numpy as jnp
from jax import lax
from jax.experimental import pallas as pl
from jax.experimental.pallas import tpu as pltpu
from jax.sharding import PartitionSpec as P

C0, C1, C2, C3, C4 = (-205.0 / 72.0, 8.0 / 5.0, -1.0 / 5.0, 8.0 / 315.0, -1.0 / 560.0)
MESH = pl.DeviceIdType.MESH
F32 = jnp.float32
SHOTS, DOM, STEPS = 8, 16, 8
HALO = 8
PLANES, ROWS = 48, 48


def chunk_of(d):
    return d + (d // 8) * (23 - 2 * d)


class Stencil:
    def __init__(self):
        lane = lax.broadcasted_iota(jnp.int32, (8, 128), 1)
        y = lane & 63
        self.low = lane < 64
        self.up = [y >= k for k in (1, 2, 3, 4)]
        self.down = [y < 64 - k for k in (1, 2, 3, 4)]

    def __call__(self, ref, z, i):
        row = 8 + 8 * i
        mid = ref[z, pl.ds(row, 8), :]
        pairs = []
        for k in (1, 2, 3, 4):
            along_z = ref[z + k, pl.ds(row, 8), :] + ref[z - k, pl.ds(row, 8), :]
            ahead = pltpu.roll(jnp.where(self.up[k - 1], mid, 0.0), 128 - k, 1)
            behind = pltpu.roll(jnp.where(self.down[k - 1], mid, 0.0), k, 1)
            pairs.append(along_z + (ahead + behind))
        up1 = ref[z, pl.ds(row + 1, 8), :]
        up2 = ref[z, pl.ds(row + 2, 8), :]
        dn1 = ref[z, pl.ds(row - 1, 8), :]
        dn2 = ref[z, pl.ds(row - 2, 8), :]
        pairs[1] = pairs[1] + (up1 + dn1)
        pairs[3] = pairs[3] + (up2 + dn2)
        odd = C1 * (jnp.where(self.low, up1, mid) + jnp.where(self.low, mid, dn1))
        odd = odd + C3 * (jnp.where(self.low, up2, up1) + jnp.where(self.low, dn1, dn2))
        total = (3.0 * C0) * mid + C1 * pairs[0] + C2 * pairs[1] + C3 * pairs[2] + C4 * pairs[3]
        return mid, total + pltpu.roll(odd, 64, 1)


def kernel(
    vel, fwd_cur, fwd_prev, adj_cur, adj_prev, rec_pos, observed, wavelet, src_pos, count, aperture, block_slot,
    out,
    v_in, v_t, v_1, v_2, picks, m_2, f_in, f_t, f_1,
    u_a, u_b, p_c, p_p, w_a, w_b, m_x, laps, res, hits, onehot, grad, land, land_m, land_p,
    g_send, g_recv, batch, batch_1, batch_t,
    in_sem, own_sem, va_s, va_r, f_s, f_r, vb_s, vb_r, vc_s, vc_r, gd_s, gd_r, gf_s, gf_r, gg_s, gg_r,
    h_s, h_r, hm_s, hm_r, hp_s, hp_r,
):
    s, d = lax.axis_index("shot"), lax.axis_index("dom")
    e = chunk_of(d)

    v_load = pltpu.make_async_copy(vel, v_in, in_sem.at[4])
    v_load.start()
    loads = []
    for f, ref in enumerate((fwd_cur, fwd_prev, adj_cur, adj_prev)):
        loads.append(pltpu.make_async_copy(ref, f_in.at[f], in_sem.at[f]))
        loads[-1].start()

    barrier = pltpu.get_barrier_semaphore()
    for o in range(1, DOM):
        pl.semaphore_signal(barrier, inc=1, device_id=(s, lax.rem(d + o, DOM)), device_id_type=MESH)
    for o in range(1, SHOTS):
        pl.semaphore_signal(barrier, inc=1, device_id=(lax.rem(s + o, SHOTS), d), device_id_type=MESH)

    def over_dom(src, dst, send, recv):
        def copy(o):
            p = lax.rem(d + o, DOM)
            return pltpu.make_async_remote_copy(
                src_ref=src(p), dst_ref=dst, send_sem=send(o), recv_sem=recv(o), device_id=(s, p), device_id_type=MESH
            )

        return copy, DOM

    def over_shot(src, dst, send, recv):
        def copy(o):
            p = lax.rem(s + o, SHOTS)
            return pltpu.make_async_remote_copy(
                src_ref=src(p), dst_ref=dst, send_sem=send(o), recv_sem=recv(o), device_id=(p, d), device_id_type=MESH
            )

        return copy, SHOTS

    def start(exchange, own):
        copy, n = exchange

        def body(o, c):
            copy(o).start()
            return c

        lax.fori_loop(1, n, body, 0)
        own.start()

    def finish(exchange, own):
        copy, n = exchange

        def body(o, c):
            copy(o).wait()
            return c

        lax.fori_loop(1, n, body, 0)
        own.wait()

    def transpose_in(src, dst):
        def body(q, c):
            for xp in range(2):
                block = src[pl.ds(2 * xp, 2), :, pl.ds(pl.multiple_of(q * 128, 128), 128)]
                dst[xp, pl.ds(q * 128, 128), :] = block.reshape(128, 128).T
            return c

        lax.fori_loop(0, 4, body, 0)

    v_load.wait()
    for slot in range(2):
        transpose_in(v_in.at[slot], v_t.at[slot])
    pl.semaphore_wait(barrier, DOM + SHOTS - 2)

    def z_of(p):
        return pl.ds(chunk_of(p) * 32, 32)

    va = over_dom(lambda p: v_t.at[:, :, z_of(p), :], v_1.at[:, d], lambda o: va_s.at[o], lambda o: va_r.at[o])
    va_own = pltpu.make_async_copy(v_t.at[:, :, z_of(d), :], v_1.at[:, d], own_sem.at[0])
    start(va, va_own)

    fields, fields_own = [], []
    for f in range(4):
        fields.append(
            over_dom(
                lambda p, f=f: f_t.at[f, :, z_of(p), :],
                f_1.at[f, pl.ds(2 * d, 2)],
                lambda o, f=f: f_s.at[f, o],
                lambda o, f=f: f_r.at[f, o],
            )
        )
        fields_own.append(pltpu.make_async_copy(f_t.at[f, :, z_of(d), :], f_1.at[f, pl.ds(2 * d, 2)], own_sem.at[1 + f]))
    for f in range(2):
        loads[f].wait()
        transpose_in(f_in.at[f], f_t.at[f])
        start(fields[f], fields_own[f])
    for f in range(2, 4):
        loads[f].wait()
        transpose_in(f_in.at[f], f_t.at[f])

    pos = rec_pos[...]
    rec_row = (((pos & 511) - 32 * e + 4) << 5) + (pos >> 16)
    rec_lane = (((pos >> 15) & 1) << 6) + ((pos >> 9) & 63)
    row_id = lax.broadcasted_iota(jnp.int32, (256, 256), 0)
    for g in range(5):
        onehot[g] = (row_id + 256 * g == rec_row).astype(F32).astype(jnp.bfloat16)
    lanes = (lax.broadcasted_iota(jnp.int32, (128, 256), 0) == rec_lane).astype(F32)

    def dot(g, b):
        found = lax.dot_general(onehot[g], b, (((1,), (1,)), ((), ())), preferred_element_type=F32)
        return found.reshape(8, 32, 128)

    ones = lanes.astype(jnp.bfloat16)
    for g in range(5):
        hits[pl.ds(8 * g, 8)] = dot(g, ones)

    def record(t, c):
        b = lanes * observed[pl.ds(t, 1), :]
        high = b.astype(jnp.bfloat16)
        low = (b - high.astype(F32)).astype(jnp.bfloat16)
        for g in range(5):
            res[t, pl.ds(8 * g, 8)] = dot(g, high) + dot(g, low)
        return c

    lax.fori_loop(0, STEPS, record, 0)

    def clear(z, c):
        for ref in (u_a, u_b, p_c, p_p, w_a, w_b, m_x):
            ref[z] = jnp.zeros((ROWS, 128), F32)
        return c

    lax.fori_loop(0, PLANES, clear, 0)

    finish(va, va_own)
    vb = over_shot(
        lambda p: v_1.at[:, :, p // 4, pl.ds(lax.rem(p, 4) * 8, 8), :],
        v_2.at[pl.ds(2 * s, 2)],
        lambda o: vb_s.at[o],
        lambda o: vb_r.at[o],
    )
    vb_own = pltpu.make_async_copy(
        v_1.at[:, :, s // 4, pl.ds(lax.rem(s, 4) * 8, 8), :], v_2.at[pl.ds(2 * s, 2)], own_sem.at[5]
    )
    start(vb, vb_own)

    def relayout(f, dst):
        flat = dst.reshape(PLANES * ROWS, 128)

        def body(r, c):
            for g in range(4):
                flat[pl.ds((HALO + 8 * g) * ROWS + 8 + r, 8, stride=ROWS), :] = f_1[f, r, pl.ds(8 * g, 8), :]
            return c

        lax.fori_loop(0, 32, body, 0)

    def halo(src, n, land_ref, send, recv):
        def ends():
            right = pltpu.make_async_remote_copy(
                src_ref=src.at[pl.ds(HALO + 32 - n, n), pl.ds(8, 32), :],
                dst_ref=land_ref.at[0],
                send_sem=send.at[0],
                recv_sem=recv.at[0],
                device_id=(s, chunk_of(lax.rem(e + 1, DOM))),
                device_id_type=MESH,
            )
            left = pltpu.make_async_remote_copy(
                src_ref=src.at[pl.ds(HALO, n), pl.ds(8, 32), :],
                dst_ref=land_ref.at[1],
                send_sem=send.at[1],
                recv_sem=recv.at[1],
                device_id=(s, chunk_of(lax.rem(e + DOM - 1, DOM))),
                device_id_type=MESH,
            )
            return right, left

        def begin():
            right, left = ends()
            pl.when(e < DOM - 1)(right.start)
            pl.when(e > 0)(left.start)

        def sent():
            right, left = ends()
            pl.when(e < DOM - 1)(right.wait_send)
            pl.when(e > 0)(left.wait_send)

        def arrived(use):
            right, left = ends()

            @pl.when(e > 0)
            def _():
                right.wait_recv()
                use(0, HALO - n)

            @pl.when(e < DOM - 1)
            def _():
                left.wait_recv()
                use(1, HALO + 32)

        return begin, sent, arrived

    def put(dst, land_ref, n):
        def use(side, at):
            def body(z, c):
                dst[at + z, pl.ds(8, 32), :] = land_ref[side, z]
                return c

            lax.fori_loop(0, n, body, 0)

        return use

    for f, dst in ((0, u_a), (1, u_b)):
        finish(fields[f], fields_own[f])
        relayout(f, dst)
    begin, sent, arrived = halo(u_b, 4, land_p.at[0], hp_s.at[0], hp_r.at[0])
    begin()

    finish(vb, vb_own)

    def pick(q, c):
        shot, k = q // 16, lax.rem(q, 16)
        block = aperture[shot, k]
        block_x = block >> 3
        slot = block_slot[((block_x >> 4) << 3) + (block & 7)]
        picks[shot, k] = v_2[slot, block_x & 15]
        return c

    lax.fori_loop(0, SHOTS * 16, pick, 0)
    vc = over_shot(lambda p: picks.at[p], m_2.at[s], lambda o: vc_s.at[o], lambda o: vc_r.at[o])
    vc_own = pltpu.make_async_copy(picks.at[s], m_2.at[s], own_sem.at[6])
    start(vc, vc_own)
    arrived(put(u_b, land_p.at[0], 4))
    sent()
    finish(vc, vc_own)
    m_flat = m_x.reshape(PLANES * ROWS, 128)

    def place(k, c):
        for xp in range(2):
            for g in range(4):
                m_flat[pl.ds((HALO + 8 * g) * ROWS + 8 + xp + 2 * k, 8, stride=ROWS), :] = m_2[4 * xp + g, k]
        return c

    lax.fori_loop(0, 16, place, 0)
    begin, sent, arrived = halo(m_x, 8, land_m, hm_s, hm_r)
    begin()
    arrived(put(m_x, land_m, 8))
    sent()
    for f in range(2, 4):
        start(fields[f], fields_own[f])

    lap_of = Stencil()
    source = src_pos[0]
    src_z = (source & 511) - 32 * e + HALO
    src_cell = ((source >> 16) << 7) + (((source >> 15) & 1) << 6) + ((source >> 9) & 63)
    cell = (lax.broadcasted_iota(jnp.int32, (8, 128), 0) << 7) + lax.broadcasted_iota(jnp.int32, (8, 128), 1)
    steps = jnp.full((8, 128), count[0], jnp.int32)

    def tile(i):
        return pl.ds(8 + 8 * i, 8)

    def forward(src, dst, lo, hi, t):
        active = steps > t

        def body(z, c):
            amount = jnp.where(z == src_z, wavelet[t], 0.0)
            for i in range(4):
                mid, lap = lap_of(src, z, i)
                inner = pl.ds(8 * i, 8)
                laps[t, z - 4, inner, :] = lap
                u = 2.0 * mid - dst[z, tile(i), :] + m_x[z, tile(i), :] * lap
                u = u + jnp.where(cell + 1024 * i == src_cell, amount, 0.0)
                dst[z, tile(i), :] = u
                res[t, z - 4, inner, :] = jnp.where(
                    active, hits[z - 4, inner, :] * u - res[t, z - 4, inner, :], 0.0
                )
            return c

        lax.fori_loop(lo, hi, body, 0)

    def fwd_pair(i, c):
        par = lax.rem(i, 2)
        begin, sent, arrived = halo(u_a, 8, land.at[par], h_s.at[par], h_r.at[par])
        begin()
        arrived(put(u_a, land.at[par], 8))
        forward(u_a, u_b, 4, 44, 2 * i)
        sent()
        forward(u_b, u_a, 8, 40, 2 * i + 1)
        return c

    lax.fori_loop(0, STEPS // 2, fwd_pair, 0)

    for f, dst in ((2, p_c), (3, p_p)):
        finish(fields[f], fields_own[f])
        relayout(f, dst)
    begin, sent, arrived = halo(p_p, 4, land_p.at[1], hp_s.at[1], hp_r.at[1])
    begin()

    active = steps > STEPS - 1

    def first(z, c):
        for i in range(4):
            inner = pl.ds(8 * i, 8)
            hit = p_c[z, tile(i), :] + res[STEPS - 1, z - 4, inner, :]
            p_c[z, tile(i), :] = hit
            w_a[z, tile(i), :] = m_x[z, tile(i), :] * hit
            grad[z - 4, inner, :] = jnp.where(active, hit * laps[STEPS - 1, z - 4, inner, :], 0.0)
        return c

    lax.fori_loop(8, 40, first, 0)

    def clear_ends(z, c):
        grad[z] = jnp.zeros((32, 128), F32)
        grad[36 + z] = jnp.zeros((32, 128), F32)
        return c

    lax.fori_loop(0, 4, clear_ends, 0)
    arrived(put(p_p, land_p.at[1], 4))
    sent()

    def backward(src, dst, lo, hi, t):
        active = steps > t
        then = steps > t - 1

        def body(z, c):
            for i in range(4):
                inner = pl.ds(8 * i, 8)
                _, lap = lap_of(src, z, i)
                hit = p_c[z, tile(i), :]
                prev = p_p[z, tile(i), :]
                cur = jnp.where(active, 2.0 * hit - prev + lap, hit)
                p_p[z, tile(i), :] = jnp.where(active, hit, prev)
                hit = cur + res[t - 1, z - 4, inner, :]
                p_c[z, tile(i), :] = hit
                dst[z, tile(i), :] = m_x[z, tile(i), :] * hit
                grad[z - 4, inner, :] = grad[z - 4, inner, :] + jnp.where(
                    then, hit * laps[t - 1, z - 4, inner, :], 0.0
                )
            return c

        lax.fori_loop(lo, hi, body, 0)

    def adj_ends(land_ref, t):
        stepped = steps > t + 1

        def use(side, at):
            def keep(z, c):
                for i in range(4):
                    p_p[z, tile(i), :] = jnp.where(stepped, p_c[z, tile(i), :], p_p[z, tile(i), :])
                return c

            near = at + 4 * (1 - side)
            lax.fori_loop(near, near + 4, keep, 0)

            def body(z, c):
                hit = land_ref[side, z]
                p_c[at + z, pl.ds(8, 32), :] = hit
                w_a[at + z, pl.ds(8, 32), :] = m_x[at + z, pl.ds(8, 32), :] * hit
                return c

            lax.fori_loop(0, 8, body, 0)

        return use

    def adj_pair(i, c):
        par = lax.rem(i, 2)
        t = STEPS - 1 - 2 * i
        begin, sent, arrived = halo(p_c, 8, land.at[par], h_s.at[par], h_r.at[par])
        begin()
        arrived(adj_ends(land.at[par], t))
        sent()
        backward(w_a, w_b, 4, 44, t)

        @pl.when(i < STEPS // 2 - 1)
        def _():
            backward(w_b, w_a, 8, 40, t - 1)

        return c

    lax.fori_loop(0, STEPS // 2, adj_pair, 0)

    g_flat = grad.reshape(40 * 32, 128)

    def gather(k, c):
        for xp in range(2):
            for g in range(4):
                g_send[4 * xp + g, k] = g_flat[pl.ds((4 + 8 * g) * 32 + xp + 2 * k, 8, stride=32), :]
        return c

    lax.fori_loop(0, 16, gather, 0)
    gd = over_shot(lambda p: g_send.at[p], g_recv.at[s], lambda o: gd_s.at[o], lambda o: gd_r.at[o])
    gd_own = pltpu.make_async_copy(g_send.at[s], g_recv.at[s], own_sem.at[7])
    start(gd, gd_own)
    finish(gd, gd_own)

    def add_up(col, c):
        sums = [jnp.zeros((8, 128), F32) for _ in range(16)]
        for shot in range(SHOTS):
            base = aperture[shot, 0]
            k = (col - (base >> 3)) & 15
            block_x = (base >> 3) + k
            slot = block_slot[((block_x >> 4) << 3) + (base & 7)]
            value = g_recv[shot, k]
            slots = jnp.full((8, 128), slot, jnp.int32)
            for j in range(16):
                sums[j] = sums[j] + jnp.where(slots == j, value, 0.0)
        for j in range(16):
            batch[j, col] = sums[j]
        return c

    lax.fori_loop(0, 16, add_up, 0)
    gf = over_shot(
        lambda p: batch.at[pl.ds(2 * p, 2)],
        batch_1.at[:, :, s // 4, pl.ds(lax.rem(s, 4) * 8, 8), :],
        lambda o: gf_s.at[o],
        lambda o: gf_r.at[o],
    )
    gf_own = pltpu.make_async_copy(
        batch.at[pl.ds(2 * s, 2)], batch_1.at[:, :, s // 4, pl.ds(lax.rem(s, 4) * 8, 8), :], own_sem.at[8]
    )
    start(gf, gf_own)
    finish(gf, gf_own)
    gg = over_dom(lambda p: batch_1.at[:, p], batch_t.at[:, :, z_of(d), :], lambda o: gg_s.at[o], lambda o: gg_r.at[o])
    gg_own = pltpu.make_async_copy(batch_1.at[:, d], batch_t.at[:, :, z_of(d), :], own_sem.at[9])
    start(gg, gg_own)
    finish(gg, gg_own)

    def back(q, c):
        cols = pl.ds(pl.multiple_of(q * 128, 128), 128)
        for slot in range(2):
            for xp in range(2):
                v_in[slot, pl.ds(2 * xp, 2), :, cols] = batch_t[slot, xp, pl.ds(q * 128, 128), :].T.reshape(2, 64, 128)
        return c

    lax.fori_loop(0, 4, back, 0)
    store = pltpu.make_async_copy(v_in, out, in_sem.at[4])
    store.start()
    store.wait()


def local(
    velocity,
    fwd_prev,
    fwd_cur,
    adj_prev,
    adj_cur,
    wavelet,
    src_pos,
    rec_pos,
    observed,
    step_count,
    aperture,
    block_slot,
    prev_batch,
    snapshot,
):
    shape = (2, 4, 64, 512)
    hbm = pl.BlockSpec(memory_space=pl.ANY)
    vmem = pl.BlockSpec(memory_space=pltpu.VMEM)
    smem = pl.BlockSpec(memory_space=pltpu.SMEM)
    field = pltpu.VMEM((PLANES, ROWS, 128), F32)
    dma = pltpu.SemaphoreType.DMA
    scratch = [
        pltpu.VMEM(shape, F32),
        pltpu.VMEM((2, 2, 512, 128), F32),
        pltpu.VMEM((2, 16, 2, 32, 128), F32),
        pltpu.VMEM((16, 16, 8, 128), F32),
        pltpu.VMEM((8, 16, 8, 128), F32),
        pltpu.VMEM((8, 16, 8, 128), F32),
        pltpu.VMEM((4, 4, 64, 512), F32),
        pltpu.VMEM((4, 2, 512, 128), F32),
        pltpu.VMEM((4, 32, 32, 128), F32),
        *[field] * 7,
        pltpu.VMEM((STEPS, 40, 32, 128), F32),
        pltpu.VMEM((STEPS, 40, 32, 128), F32),
        pltpu.VMEM((40, 32, 128), F32),
        pltpu.VMEM((5, 256, 256), jnp.bfloat16),
        pltpu.VMEM((40, 32, 128), F32),
        pltpu.VMEM((2, 2, 8, 32, 128), F32),
        pltpu.VMEM((2, 8, 32, 128), F32),
        pltpu.VMEM((2, 2, 4, 32, 128), F32),
        pltpu.VMEM((8, 16, 8, 128), F32),
        pltpu.VMEM((8, 16, 8, 128), F32),
        pltpu.VMEM((16, 16, 8, 128), F32),
        pltpu.VMEM((2, 16, 2, 32, 128), F32),
        pltpu.VMEM((2, 2, 512, 128), F32),
        dma((5,)),
        dma((10,)),
        dma((16,)), dma((16,)),
        dma((4, 16)), dma((4, 16)),
        dma((8,)), dma((8,)),
        dma((8,)), dma((8,)),
        dma((8,)), dma((8,)),
        dma((8,)), dma((8,)),
        dma((16,)), dma((16,)),
        dma((2, 2)), dma((2, 2)),
        dma((2,)), dma((2,)),
        dma((2, 2)), dma((2, 2)),
    ]
    batch = pl.pallas_call(
        kernel,
        out_shape=jax.ShapeDtypeStruct(shape, F32),
        in_specs=[hbm] * 5 + [vmem] * 2 + [smem] * 5,
        out_specs=hbm,
        scratch_shapes=scratch,
        name="adjoint_gradient",
        compiler_params=pltpu.CompilerParams(collective_id=0, has_side_effects=True, vmem_limit_bytes=56 << 20),
    )(
        velocity.reshape(shape),
        fwd_cur[0],
        fwd_prev[0],
        adj_cur[0],
        adj_prev[0],
        rec_pos,
        observed[0],
        wavelet[0],
        src_pos,
        step_count,
        aperture,
        block_slot,
    )
    result = (batch - prev_batch.reshape(shape)) + snapshot.reshape(shape)
    return result.reshape(velocity.shape)


def solution(mesh):
    placed = (
        P("shot", "dom", None, None, None),
        P("shot", "dom", None, None),
        P("shot", "dom", None, None),
        P("shot", "dom", None, None),
        P("shot", "dom", None, None),
        P("shot", None),
        P("shot"),
        P("shot", None),
        P("shot", None, None),
        P("shot"),
        P(),
        P(),
        P("shot", "dom", None, None, None),
        P("shot", "dom", None, None, None),
    )
    return jax.shard_map(
        local,
        mesh=mesh,
        in_specs=placed,
        out_specs=P("shot", "dom", None, None, None),
        check_vma=False,
    )
```

```python
import functools

import jax
import jax.numpy as jnp
from jax import lax
from jax.experimental import pallas as pl
from jax.experimental.pallas import tpu as pltpu
from jax.sharding import PartitionSpec as P

C0, C1, C2, C3, C4 = (-205.0 / 72.0, 8.0 / 5.0, -1.0 / 5.0, 8.0 / 315.0, -1.0 / 560.0)
MESH = pl.DeviceIdType.MESH
F32 = jnp.float32
SHOTS, DOM, STEPS = 8, 16, 8
HALO = 8
PLANES, ROWS = 48, 48


def chunk_of(d):
    return d + (d // 8) * (23 - 2 * d)


def band():
    row = lax.broadcasted_iota(jnp.int32, (256, 256), 0)
    col = lax.broadcasted_iota(jnp.int32, (256, 256), 1)
    gap = jnp.abs((row & 127) - (col & 127))
    same = ((row >> 6) & 1) == ((col >> 6) & 1)
    full = jnp.zeros((256, 256), F32)
    for k, c in ((1, C1), (2, C2), (3, C3), (4, C4)):
        full = full + jnp.where(same & (gap == k), c, 0.0)
    high = full.astype(jnp.bfloat16).astype(F32)
    low = jnp.where(row < 128, full - high, 0.0)
    return jnp.where(col < 128, high, low).astype(jnp.bfloat16)


def stencil(ref, z0, weights):
    low = lax.broadcasted_iota(jnp.int32, (8, 128), 1) < 64
    cells = jnp.concatenate([ref[z0 + p, pl.ds(8, 32), :] for p in range(8)], 0)
    high = cells.astype(jnp.bfloat16)
    rest = (cells - high.astype(F32)).astype(jnp.bfloat16)
    along_y = jnp.dot(jnp.concatenate([high, rest], 1), weights, preferred_element_type=F32)
    along_y = along_y[:, :128] + along_y[:, 128:]
    for p in range(8):
        z = z0 + p
        for i in range(4):
            row = 8 + 8 * i
            mid = ref[z, pl.ds(row, 8), :]
            pairs = [ref[z + k, pl.ds(row, 8), :] + ref[z - k, pl.ds(row, 8), :] for k in (1, 2, 3, 4)]
            up1, up2, dn1, dn2 = (ref[z, pl.ds(row + k, 8), :] for k in (1, 2, -1, -2))
            pairs[1] = pairs[1] + (up1 + dn1)
            pairs[3] = pairs[3] + (up2 + dn2)
            odd = C1 * (jnp.where(low, up1, mid) + jnp.where(low, mid, dn1))
            odd = odd + C3 * (jnp.where(low, up2, up1) + jnp.where(low, dn1, dn2))
            total = (3.0 * C0) * mid + C1 * pairs[0] + C2 * pairs[1] + C3 * pairs[2] + C4 * pairs[3]
            lap = total + pltpu.roll(odd, 64, 1) + along_y[32 * p + 8 * i : 32 * p + 8 * i + 8]
            yield z, i, mid, lap


def kernel(
    vel, fwd_cur, fwd_prev, adj_cur, adj_prev, rec_pos, observed, wavelet, src_pos, count, aperture, block_slot,
    out,
    v_2, picks, m_b, m_t, m_1, f_in, f_t, f_1,
    u_a, u_b, p_a, p_b, p_p, w_a, w_b, m_x, laps, res, hits, onehot, weights, grad, land, land_m, land_p,
    g_1, g_send, g_t, g_b, g_recv, batch,
    in_sem, own_sem, va_s, va_r, f_s, f_r, vb_s, vb_r, vc_s, vc_r, gd_s, gd_r, gf_s, gf_r, gg_s, gg_r,
    h_s, h_r, hm_s, hm_r, hp_s, hp_r,
):
    s, d = lax.axis_index("shot"), lax.axis_index("dom")
    e = chunk_of(d)

    loads = []
    for f, ref in enumerate((fwd_cur, fwd_prev, adj_cur, adj_prev)):
        loads.append(pltpu.make_async_copy(ref, f_in.at[f], in_sem.at[f]))
        loads[-1].start()

    barrier = pltpu.get_barrier_semaphore()
    for o in range(1, DOM):
        pl.semaphore_signal(barrier, inc=1, device_id=(s, lax.rem(d + o, DOM)), device_id_type=MESH)
    for o in range(1, SHOTS):
        pl.semaphore_signal(barrier, inc=1, device_id=(lax.rem(s + o, SHOTS), d), device_id_type=MESH)

    def over_dom(src, dst, send, recv):
        def copy(o):
            p = lax.rem(d + o, DOM)
            return pltpu.make_async_remote_copy(
                src_ref=src(p), dst_ref=dst, send_sem=send(o), recv_sem=recv(o), device_id=(s, p), device_id_type=MESH
            )

        return copy, DOM

    def over_shot(src, dst, send, recv):
        def copy(o):
            p = lax.rem(s + o, SHOTS)
            return pltpu.make_async_remote_copy(
                src_ref=src(p), dst_ref=dst, send_sem=send(o), recv_sem=recv(o), device_id=(p, d), device_id_type=MESH
            )

        return copy, SHOTS

    def start(exchange, own):
        copy, n = exchange

        def body(o, c):
            copy(o).start()
            return c

        lax.fori_loop(1, n, body, 0)
        own.start()

    def finish(exchange, own):
        copy, n = exchange

        def body(o, c):
            copy(o).wait()
            return c

        lax.fori_loop(1, n, body, 0)
        own.wait()

    def transpose_in(src, dst):
        def body(q, c):
            for xp in range(2):
                block = src[pl.ds(2 * xp, 2), :, pl.ds(pl.multiple_of(q * 128, 128), 128)]
                dst[xp, pl.ds(q * 128, 128), :] = block.reshape(128, 128).T
            return c

        lax.fori_loop(0, 4, body, 0)

    def z_of(p):
        return pl.ds(chunk_of(p) * 32, 32)

    def rows_of(p):
        return pl.ds(p * 8, 8)

    loads[0].wait()
    transpose_in(f_in.at[0], f_t.at[0])
    pl.semaphore_wait(barrier, DOM + SHOTS - 2)
    va = over_shot(
        lambda p: vel.at[:, :, rows_of(p), :], v_2.at[pl.ds(2 * s, 2)], lambda o: va_s.at[o], lambda o: va_r.at[o]
    )
    va_own = pltpu.make_async_copy(vel.at[:, :, rows_of(s), :], v_2.at[pl.ds(2 * s, 2)], own_sem.at[0])
    start(va, va_own)

    fields, fields_own = [], []
    for f in range(4):
        fields.append(
            over_dom(
                lambda p, f=f: f_t.at[f, :, z_of(p), :],
                f_1.at[f, pl.ds(2 * d, 2)],
                lambda o, f=f: f_s.at[f, o],
                lambda o, f=f: f_r.at[f, o],
            )
        )
        fields_own.append(pltpu.make_async_copy(f_t.at[f, :, z_of(d), :], f_1.at[f, pl.ds(2 * d, 2)], own_sem.at[1 + f]))
    start(fields[0], fields_own[0])
    loads[1].wait()
    transpose_in(f_in.at[1], f_t.at[1])
    start(fields[1], fields_own[1])
    for f in range(2, 4):
        loads[f].wait()
        transpose_in(f_in.at[f], f_t.at[f])

    pos = rec_pos[...]
    rec_row = (((pos & 511) - 32 * e + 4) << 5) + (pos >> 16)
    rec_lane = (((pos >> 15) & 1) << 6) + ((pos >> 9) & 63)
    row_id = lax.broadcasted_iota(jnp.int32, (256, 256), 0)
    for g in range(5):
        onehot[g] = (row_id + 256 * g == rec_row).astype(F32).astype(jnp.bfloat16)
    lanes = (lax.broadcasted_iota(jnp.int32, (128, 256), 0) == rec_lane).astype(F32)

    def dot(g, b):
        found = lax.dot_general(onehot[g], b, (((1,), (1,)), ((), ())), preferred_element_type=F32)
        return found.reshape(8, 32, 128)

    ones = lanes.astype(jnp.bfloat16)
    for g in range(5):
        hits[pl.ds(8 * g, 8)] = dot(g, ones)

    def record(t, c):
        b = lanes * observed[pl.ds(t, 1), :]
        high = b.astype(jnp.bfloat16)
        low = (b - high.astype(F32)).astype(jnp.bfloat16)
        for g in range(5):
            res[t, pl.ds(8 * g, 8)] = dot(g, high) + dot(g, low)
        return c

    lax.fori_loop(0, STEPS, record, 0)

    def clear(z, c):
        for ref in (u_a, u_b, p_a, p_b, p_p, w_a, w_b, m_x):
            ref[z] = jnp.zeros((ROWS, 128), F32)
        return c

    lax.fori_loop(0, PLANES, clear, 0)
    weights[...] = band()

    finish(va, va_own)

    def slot_of(shot, col):
        first = aperture[shot, 0]
        block_x = (first >> 3) + ((col - (first >> 3)) & 15)
        return block_slot[((block_x >> 4) << 3) + (first & 7)]

    def pick(shot, c):
        picks[shot] = v_2[slot_of(shot, d)]
        return c

    lax.fori_loop(0, SHOTS, pick, 0)
    vb = over_shot(lambda p: picks.at[p], m_b.at[:, rows_of(s), :], lambda o: vb_s.at[o], lambda o: vb_r.at[o])
    vb_own = pltpu.make_async_copy(picks.at[s], m_b.at[:, rows_of(s), :], own_sem.at[5])
    start(vb, vb_own)

    def relayout(f, dst):
        flat = dst.reshape(PLANES * ROWS, 128)

        def body(r, c):
            for g in range(4):
                flat[pl.ds((HALO + 8 * g) * ROWS + 8 + r, 8, stride=ROWS), :] = f_1[f, r, pl.ds(8 * g, 8), :]
            return c

        lax.fori_loop(0, 32, body, 0)

    def halo(src, n, land_ref, send, recv):
        def ends():
            right = pltpu.make_async_remote_copy(
                src_ref=src.at[pl.ds(HALO + 32 - n, n), pl.ds(8, 32), :],
                dst_ref=land_ref.at[0],
                send_sem=send.at[0],
                recv_sem=recv.at[0],
                device_id=(s, chunk_of(lax.rem(e + 1, DOM))),
                device_id_type=MESH,
            )
            left = pltpu.make_async_remote_copy(
                src_ref=src.at[pl.ds(HALO, n), pl.ds(8, 32), :],
                dst_ref=land_ref.at[1],
                send_sem=send.at[1],
                recv_sem=recv.at[1],
                device_id=(s, chunk_of(lax.rem(e + DOM - 1, DOM))),
                device_id_type=MESH,
            )
            return right, left

        def begin():
            right, left = ends()
            pl.when(e < DOM - 1)(right.start)
            pl.when(e > 0)(left.start)

        def sent():
            right, left = ends()
            pl.when(e < DOM - 1)(right.wait_send)
            pl.when(e > 0)(left.wait_send)

        def arrived(use):
            right, left = ends()

            @pl.when(e > 0)
            def _():
                right.wait_recv()
                use(0, HALO - n)

            @pl.when(e < DOM - 1)
            def _():
                left.wait_recv()
                use(1, HALO + 32)

        return begin, sent, arrived

    def put(dst, land_ref, n):
        def use(side, at):
            def body(z, c):
                dst[at + z, pl.ds(8, 32), :] = land_ref[side, z]
                return c

            lax.fori_loop(0, n, body, 0)

        return use

    def u_halo(par):
        return halo(u_a, 8, land.at[par], h_s.at[par], h_r.at[par])

    finish(fields[0], fields_own[0])
    relayout(0, u_a)
    u_halo(0)[0]()
    finish(fields[1], fields_own[1])
    relayout(1, u_b)
    prev_halo = halo(u_b, 4, land_p.at[0], hp_s.at[0], hp_r.at[0])
    prev_halo[0]()

    finish(vb, vb_own)
    transpose_in(m_b, m_t)
    vc = over_dom(lambda p: m_t.at[:, z_of(p), :], m_1.at[d], lambda o: vc_s.at[o], lambda o: vc_r.at[o])
    vc_own = pltpu.make_async_copy(m_t.at[:, z_of(d), :], m_1.at[d], own_sem.at[6])
    start(vc, vc_own)
    prev_halo[2](put(u_b, land_p.at[0], 4))
    prev_halo[1]()
    finish(vc, vc_own)
    for f in range(2, 4):
        start(fields[f], fields_own[f])
    m_flat = m_x.reshape(PLANES * ROWS, 128)
    base_x = aperture[s, 0] >> 3

    def place(k, c):
        slab = m_1[(base_x + k) & 15]
        for xp in range(2):
            for g in range(4):
                m_flat[pl.ds((HALO + 8 * g) * ROWS + 8 + xp + 2 * k, 8, stride=ROWS), :] = slab[xp, 8 * g : 8 * g + 8]
        return c

    lax.fori_loop(0, 16, place, 0)
    model_halo = halo(m_x, 8, land_m, hm_s, hm_r)
    model_halo[0]()

    source = src_pos[0]
    src_z = (source & 511) - 32 * e + HALO
    src_cell = ((source >> 16) << 7) + (((source >> 15) & 1) << 6) + ((source >> 9) & 63)
    cell = (lax.broadcasted_iota(jnp.int32, (8, 128), 0) << 7) + lax.broadcasted_iota(jnp.int32, (8, 128), 1)
    steps = jnp.full((8, 128), count[0], jnp.int32)

    def tile(i):
        return pl.ds(8 + 8 * i, 8)

    def inner(i):
        return pl.ds(8 * i, 8)

    def blocks(body, first, stride, n):
        def one(j, c):
            body(first + stride * j)
            return c

        lax.fori_loop(0, n, one, 0)

    def forward(src, dst, t):
        def body(z0):
            active = steps > t
            found = []
            for z, i, mid, lap in stencil(src, z0, weights[...]):
                amount = jnp.where(z == src_z, wavelet[t], 0.0)
                u = 2.0 * mid - dst[z, tile(i), :] + m_x[z, tile(i), :] * lap
                u = u + jnp.where(cell + 1024 * i == src_cell, amount, 0.0)
                miss = jnp.where(active, hits[z - 4, inner(i), :] * u - res[t, z - 4, inner(i), :], 0.0)
                found.append((z, i, lap, u, miss))
            for z, i, lap, u, miss in found:
                laps[t, z - 4, inner(i), :] = lap
                dst[z, tile(i), :] = u
                res[t, z - 4, inner(i), :] = miss

        return body

    def fwd_pair(i, c):
        par, then = lax.rem(i, 2), lax.rem(i + 1, 2)
        step = forward(u_a, u_b, 2 * i)
        blocks(step, 12, 8, 3)

        @pl.when(i == 0)
        def _():
            model_halo[2](put(m_x, land_m, 8))
            model_halo[1]()

        u_halo(par)[2](put(u_a, land.at[par], 8))
        blocks(step, 4, 32, 2)
        u_halo(par)[1]()
        step = forward(u_b, u_a, 2 * i + 1)
        blocks(step, 8, 24, 2)
        pl.when(i < STEPS // 2 - 1)(u_halo(then)[0])
        blocks(step, 16, 8, 2)
        return c

    lax.fori_loop(0, 2, fwd_pair, 0)
    for f, dst in ((2, p_a), (3, p_p)):
        finish(fields[f], fields_own[f])
        relayout(f, dst)
    prev_halo = halo(p_p, 4, land_p.at[1], hp_s.at[1], hp_r.at[1])
    prev_halo[0]()
    lax.fori_loop(2, STEPS // 2, fwd_pair, 0)
    prev_halo[2](put(p_p, land_p.at[1], 4))
    prev_halo[1]()

    def p_halo(par):
        return halo(p_a, 8, land.at[par], h_s.at[par], h_r.at[par])

    def first(z, c):
        active = steps > STEPS - 1
        found = []
        for i in range(4):
            hit = p_a[z, tile(i), :] + res[STEPS - 1, z - 4, inner(i), :]
            part = jnp.where(active, hit * laps[STEPS - 1, z - 4, inner(i), :], 0.0)
            found.append((i, hit, m_x[z, tile(i), :] * hit, part))
        for i, hit, w, part in found:
            p_a[z, tile(i), :] = hit
            w_a[z, tile(i), :] = w
            grad[z - 4, inner(i), :] = part
        return c

    lax.fori_loop(8, 16, first, 0)
    lax.fori_loop(32, 40, first, 0)
    p_halo(0)[0]()
    lax.fori_loop(16, 32, first, 0)

    def clear_ends(z, c):
        grad[z] = jnp.zeros((32, 128), F32)
        grad[36 + z] = jnp.zeros((32, 128), F32)
        return c

    lax.fori_loop(0, 4, clear_ends, 0)

    def backward(src, dst, p_now, p_then, t):
        def body(z0):
            active, then = steps > t, steps > t - 1
            found = []
            for z, i, _, lap in stencil(src, z0, weights[...]):
                hit = p_now[z, tile(i), :]
                prev = p_p[z, tile(i), :]
                cur = jnp.where(active, 2.0 * hit - prev + lap, hit)
                prev = jnp.where(active, hit, prev)
                hit = cur + res[t - 1, z - 4, inner(i), :]
                part = jnp.where(then, hit * laps[t - 1, z - 4, inner(i), :], 0.0)
                found.append((z, i, prev, hit, m_x[z, tile(i), :] * hit, grad[z - 4, inner(i), :] + part))
            for z, i, prev, hit, w, total in found:
                p_p[z, tile(i), :] = prev
                p_then[z, tile(i), :] = hit
                dst[z, tile(i), :] = w
                grad[z - 4, inner(i), :] = total

        return body

    def adj_ends(land_ref, t):
        stepped = steps > t + 1

        def use(side, at):
            near = at + 4 * (1 - side)

            def keep(z, c):
                for i in range(4):
                    p_p[z, tile(i), :] = jnp.where(stepped, p_b[z, tile(i), :], p_p[z, tile(i), :])
                return c

            lax.fori_loop(near, near + 4, keep, 0)

            def body(z, c):
                hit = land_ref[side, z]
                p_a[at + z, pl.ds(8, 32), :] = hit
                w_a[at + z, pl.ds(8, 32), :] = m_x[at + z, pl.ds(8, 32), :] * hit
                return c

            lax.fori_loop(0, 8, body, 0)

        return use

    def adj_pair(i, c):
        par, then = lax.rem(i, 2), lax.rem(i + 1, 2)
        t = STEPS - 1 - 2 * i
        step = backward(w_a, w_b, p_a, p_b, t)
        blocks(step, 12, 8, 3)
        p_halo(par)[2](adj_ends(land.at[par], t))
        blocks(step, 4, 32, 2)
        p_halo(par)[1]()

        @pl.when(i < STEPS // 2 - 1)
        def _():
            step = backward(w_b, w_a, p_b, p_a, t - 1)
            blocks(step, 8, 24, 2)
            p_halo(then)[0]()
            blocks(step, 16, 8, 2)

        return c

    lax.fori_loop(0, STEPS // 2, adj_pair, 0)

    g_flat = grad.reshape(40 * 32, 128)

    def gather(k, c):
        for xp in range(2):
            for g in range(4):
                g_1[k, xp, pl.ds(8 * g, 8), :] = g_flat[pl.ds((4 + 8 * g) * 32 + xp + 2 * k, 8, stride=32), :]
        return c

    lax.fori_loop(0, 16, gather, 0)

    def turn(col, c):
        g_send[col] = g_1[(col - base_x) & 15]
        return c

    lax.fori_loop(0, 16, turn, 0)
    gd = over_dom(lambda p: g_send.at[p], g_t.at[:, z_of(d), :], lambda o: gd_s.at[o], lambda o: gd_r.at[o])
    gd_own = pltpu.make_async_copy(g_send.at[d], g_t.at[:, z_of(d), :], own_sem.at[7])
    start(gd, gd_own)
    finish(gd, gd_own)

    def back(q, c):
        cols = pl.ds(pl.multiple_of(q * 128, 128), 128)
        for xp in range(2):
            g_b[pl.ds(2 * xp, 2), :, cols] = g_t[xp, pl.ds(q * 128, 128), :].T.reshape(2, 64, 128)
        return c

    lax.fori_loop(0, 4, back, 0)
    gf = over_shot(lambda p: g_b.at[:, rows_of(p), :], g_recv.at[s], lambda o: gf_s.at[o], lambda o: gf_r.at[o])
    gf_own = pltpu.make_async_copy(g_b.at[:, rows_of(s), :], g_recv.at[s], own_sem.at[8])
    start(gf, gf_own)
    finish(gf, gf_own)
    owners = [jnp.full((8, 128), slot_of(shot, d), jnp.int32) for shot in range(SHOTS)]

    def add_up(slot, c):
        mine = [owner == slot for owner in owners]
        sums = []
        for x in range(4):
            for q in range(4):
                total = jnp.zeros((8, 128), F32)
                for shot in range(SHOTS):
                    total = total + jnp.where(mine[shot], g_recv[shot, x, :, pl.ds(128 * q, 128)], 0.0)
                sums.append((x, q, total))
        for x, q, total in sums:
            batch[slot, x, :, pl.ds(128 * q, 128)] = total
        return c

    lax.fori_loop(0, 16, add_up, 0)
    gg = over_shot(
        lambda p: batch.at[pl.ds(2 * p, 2)], out.at[:, :, rows_of(s), :], lambda o: gg_s.at[o], lambda o: gg_r.at[o]
    )
    gg_own = pltpu.make_async_copy(batch.at[pl.ds(2 * s, 2)], out.at[:, :, rows_of(s), :], own_sem.at[9])
    start(gg, gg_own)
    finish(gg, gg_own)


def local(
    velocity,
    fwd_prev,
    fwd_cur,
    adj_prev,
    adj_cur,
    wavelet,
    src_pos,
    rec_pos,
    observed,
    step_count,
    aperture,
    block_slot,
    prev_batch,
    snapshot,
):
    shape = (2, 4, 64, 512)
    hbm = pl.BlockSpec(memory_space=pl.ANY)
    vmem = pl.BlockSpec(memory_space=pltpu.VMEM)
    smem = pl.BlockSpec(memory_space=pltpu.SMEM)
    field = pltpu.VMEM((PLANES, ROWS, 128), F32)
    dma = pltpu.SemaphoreType.DMA
    scratch = [
        pltpu.VMEM((16, 4, 8, 512), F32),
        pltpu.VMEM((8, 4, 8, 512), F32),
        pltpu.VMEM((4, 64, 512), F32),
        pltpu.VMEM((2, 512, 128), F32),
        pltpu.VMEM((16, 2, 32, 128), F32),
        pltpu.VMEM((4, 4, 64, 512), F32),
        pltpu.VMEM((4, 2, 512, 128), F32),
        pltpu.VMEM((4, 32, 32, 128), F32),
        *[field] * 8,
        pltpu.VMEM((STEPS, 40, 32, 128), F32),
        pltpu.VMEM((STEPS, 40, 32, 128), F32),
        pltpu.VMEM((40, 32, 128), F32),
        pltpu.VMEM((5, 256, 256), jnp.bfloat16),
        pltpu.VMEM((256, 256), jnp.bfloat16),
        pltpu.VMEM((40, 32, 128), F32),
        pltpu.VMEM((2, 2, 8, 32, 128), F32),
        pltpu.VMEM((2, 8, 32, 128), F32),
        pltpu.VMEM((2, 2, 4, 32, 128), F32),
        pltpu.VMEM((16, 2, 32, 128), F32),
        pltpu.VMEM((16, 2, 32, 128), F32),
        pltpu.VMEM((2, 512, 128), F32),
        pltpu.VMEM((4, 64, 512), F32),
        pltpu.VMEM((8, 4, 8, 512), F32),
        pltpu.VMEM((16, 4, 8, 512), F32),
        dma((4,)),
        dma((10,)),
        dma((8,)), dma((8,)),
        dma((4, 16)), dma((4, 16)),
        dma((8,)), dma((8,)),
        dma((16,)), dma((16,)),
        dma((16,)), dma((16,)),
        dma((8,)), dma((8,)),
        dma((8,)), dma((8,)),
        dma((2, 2)), dma((2, 2)),
        dma((2,)), dma((2,)),
        dma((2, 2)), dma((2, 2)),
    ]
    batch = pl.pallas_call(
        kernel,
        out_shape=jax.ShapeDtypeStruct(shape, F32),
        in_specs=[hbm] * 5 + [vmem] * 2 + [smem] * 5,
        out_specs=hbm,
        scratch_shapes=scratch,
        name="adjoint_gradient",
        compiler_params=pltpu.CompilerParams(collective_id=0, has_side_effects=True, vmem_limit_bytes=56 << 20),
    )(
        velocity.reshape(shape),
        fwd_cur[0],
        fwd_prev[0],
        adj_cur[0],
        adj_prev[0],
        rec_pos,
        observed[0],
        wavelet[0],
        src_pos,
        step_count,
        aperture,
        block_slot,
    )
    result = (batch - prev_batch.reshape(shape)) + snapshot.reshape(shape)
    return result.reshape(velocity.shape)


def solution(mesh):
    placed = (
        P("shot", "dom", None, None, None),
        P("shot", "dom", None, None),
        P("shot", "dom", None, None),
        P("shot", "dom", None, None),
        P("shot", "dom", None, None),
        P("shot", None),
        P("shot"),
        P("shot", None),
        P("shot", None, None),
        P("shot"),
        P(),
        P(),
        P("shot", "dom", None, None, None),
        P("shot", "dom", None, None, None),
    )
    return jax.shard_map(
        local,
        mesh=mesh,
        in_specs=placed,
        out_specs=P("shot", "dom", None, None, None),
        check_vma=False,
    )
```

```python
import functools

import jax
import jax.numpy as jnp
from jax import lax
from jax.experimental import pallas as pl
from jax.experimental.pallas import tpu as pltpu
from jax.sharding import PartitionSpec as P

C0, C1, C2, C3, C4 = (-205.0 / 72.0, 8.0 / 5.0, -1.0 / 5.0, 8.0 / 315.0, -1.0 / 560.0)
MESH = pl.DeviceIdType.MESH
F32 = jnp.float32
SHOTS, DOM, STEPS = 8, 16, 8
HALO = 8
PLANES, ROWS = 48, 48


def chunk_of(d):
    return d + (d // 8) * (23 - 2 * d)


def band():
    row = lax.broadcasted_iota(jnp.int32, (256, 256), 0)
    col = lax.broadcasted_iota(jnp.int32, (256, 256), 1)
    gap = jnp.abs((row & 127) - (col & 127))
    same = ((row >> 6) & 1) == ((col >> 6) & 1)
    full = jnp.zeros((256, 256), F32)
    for k, c in ((1, C1), (2, C2), (3, C3), (4, C4)):
        full = full + jnp.where(same & (gap == k), c, 0.0)
    high = full.astype(jnp.bfloat16).astype(F32)
    low = jnp.where(row < 128, full - high, 0.0)
    return jnp.where(col < 128, high, low).astype(jnp.bfloat16)


def stencil(ref, z0, weights):
    low = lax.broadcasted_iota(jnp.int32, (8, 128), 1) < 64
    cells = jnp.concatenate([ref[z0 + p, pl.ds(8, 32), :] for p in range(8)], 0)
    high = cells.astype(jnp.bfloat16)
    rest = (cells - high.astype(F32)).astype(jnp.bfloat16)
    along_y = jnp.dot(jnp.concatenate([high, rest], 1), weights, preferred_element_type=F32)
    along_y = along_y[:, :128] + along_y[:, 128:]
    for p in range(8):
        z = z0 + p
        for i in range(4):
            row = 8 + 8 * i
            mid = ref[z, pl.ds(row, 8), :]
            pairs = [ref[z + k, pl.ds(row, 8), :] + ref[z - k, pl.ds(row, 8), :] for k in (1, 2, 3, 4)]
            up1, up2, dn1, dn2 = (ref[z, pl.ds(row + k, 8), :] for k in (1, 2, -1, -2))
            pairs[1] = pairs[1] + (up1 + dn1)
            pairs[3] = pairs[3] + (up2 + dn2)
            odd = C1 * (jnp.where(low, up1, mid) + jnp.where(low, mid, dn1))
            odd = odd + C3 * (jnp.where(low, up2, up1) + jnp.where(low, dn1, dn2))
            total = (3.0 * C0) * mid + C1 * pairs[0] + C2 * pairs[1] + C3 * pairs[2] + C4 * pairs[3]
            lap = total + pltpu.roll(odd, 64, 1) + along_y[32 * p + 8 * i : 32 * p + 8 * i + 8]
            yield z, i, mid, lap


def kernel(
    vel, fwd_cur, fwd_prev, adj_cur, adj_prev, rec_pos, observed, wavelet, src_pos, count, aperture, block_slot,
    out,
    v_2, picks, m_b, m_t, m_1, f_in, f_t, f_1,
    u_a, u_b, p_a, p_b, p_p, w_a, w_b, m_x, laps, res, hits, onehot, weights, grad, land, land_m, land_p,
    g_1, g_send, g_t, g_b, g_recv, batch,
    in_sem, own_sem, va_s, va_r, f_s, f_r, vb_s, vb_r, vc_s, vc_r, gd_s, gd_r, gf_s, gf_r, gg_s, gg_r,
    h_s, h_r, hm_s, hm_r, hp_s, hp_r,
):
    s, d = lax.axis_index("shot"), lax.axis_index("dom")
    e = chunk_of(d)
    x, half_id = s // 2, lax.rem(s, 2)

    loads = []
    for f, ref in enumerate((fwd_cur, fwd_prev, adj_cur, adj_prev)):
        loads.append(pltpu.make_async_copy(ref, f_in.at[f], in_sem.at[f]))
        loads[-1].start()

    barrier = pltpu.get_barrier_semaphore()
    for o in range(1, DOM):
        pl.semaphore_signal(barrier, inc=1, device_id=(s, lax.rem(d + o, DOM)), device_id_type=MESH)
    for o in range(1, SHOTS):
        pl.semaphore_signal(barrier, inc=1, device_id=(lax.rem(s + o, SHOTS), d), device_id_type=MESH)

    def partner(o):
        return lax.rem(d // 8 + o // 8, 2) * 8 + lax.rem(d + o, 8)

    def over_dom(src, dst, send, recv):
        def copy(o):
            p = partner(o)
            return pltpu.make_async_remote_copy(
                src_ref=src(p), dst_ref=dst, send_sem=send(o), recv_sem=recv(o), device_id=(s, p), device_id_type=MESH
            )

        return copy, DOM

    def over_shot(src, dst, send, recv):
        def copy(o):
            p = lax.rem(s + o, SHOTS)
            return pltpu.make_async_remote_copy(
                src_ref=src(p), dst_ref=dst, send_sem=send(o), recv_sem=recv(o), device_id=(p, d), device_id_type=MESH
            )

        return copy, SHOTS

    def over_x(src, dst, send, recv):
        def copy(o):
            p = lax.rem(s + 2 * o, SHOTS)
            return pltpu.make_async_remote_copy(
                src_ref=src(p), dst_ref=dst, send_sem=send(o), recv_sem=recv(o), device_id=(p, d), device_id_type=MESH
            )

        return copy, SHOTS // 2

    def start(exchange, own):
        copy, n = exchange

        def body(o, c):
            copy(n - o).start()
            return c

        lax.fori_loop(1, n, body, 0)
        own.start()

    def finish(exchange, own):
        copy, n = exchange

        def body(o, c):
            copy(o).wait()
            return c

        lax.fori_loop(1, n, body, 0)
        own.wait()

    def transpose_pair(src, dst, xp):
        def body(q, c):
            block = src[pl.ds(2 * xp, 2), :, pl.ds(pl.multiple_of(q * 128, 128), 128)]
            dst[xp, pl.ds(q * 128, 128), :] = block.reshape(128, 128).T
            return c

        lax.fori_loop(0, 4, body, 0)

    def transpose_in(src, dst):
        for xp in range(2):
            transpose_pair(src, dst, xp)

    def z_of(p):
        return pl.ds(chunk_of(p) * 32, 32)

    def rows_of(p):
        return pl.ds(p * 8, 8)

    def quarter(p):
        return pl.ds((p // 2) * 16, 16)

    loads[0].wait()
    transpose_in(f_in.at[0], f_t.at[0])
    pl.semaphore_wait(barrier, DOM + SHOTS - 2)
    va = over_x(lambda p: vel.at[:, :, quarter(p), :], v_2.at[pl.ds(2 * x, 2)], lambda o: va_s.at[o], lambda o: va_r.at[o])
    va_own = pltpu.make_async_copy(vel.at[:, :, quarter(s), :], v_2.at[pl.ds(2 * x, 2)], own_sem.at[0, 0])
    start(va, va_own)

    fields, fields_own = [], []
    for f in range(4):
        fields.append(
            over_dom(
                lambda p, f=f: f_t.at[f, :, z_of(p), :],
                f_1.at[f, pl.ds(2 * d, 2)],
                lambda o, f=f: f_s.at[f, o],
                lambda o, f=f: f_r.at[f, o],
            )
        )
        fields_own.append(pltpu.make_async_copy(f_t.at[f, :, z_of(d), :], f_1.at[f, pl.ds(2 * d, 2)], own_sem.at[1 + f, 0]))
    start(fields[0], fields_own[0])
    loads[1].wait()
    transpose_in(f_in.at[1], f_t.at[1])
    start(fields[1], fields_own[1])
    for f in range(2, 4):
        loads[f].wait()
        transpose_in(f_in.at[f], f_t.at[f])

    def send_adjoint(lo, hi):
        for f in range(2, 4):

            def body(o, c, f=f):
                fields[f][0](o).start()
                return c

            lax.fori_loop(lo, hi, body, 0)

    for f in range(2, 4):
        fields_own[f].start()
    send_adjoint(8, 10)

    pos = rec_pos[...]
    rec_row = (((pos & 511) - 32 * e + 4) << 5) + (pos >> 16)
    rec_lane = (((pos >> 15) & 1) << 6) + ((pos >> 9) & 63)
    row_id = lax.broadcasted_iota(jnp.int32, (256, 256), 0)
    for g in range(5):
        onehot[g] = (row_id + 256 * g == rec_row).astype(F32).astype(jnp.bfloat16)
    lanes = (lax.broadcasted_iota(jnp.int32, (128, 256), 0) == rec_lane).astype(F32)

    def dot(g, b):
        found = lax.dot_general(onehot[g], b, (((1,), (1,)), ((), ())), preferred_element_type=F32)
        return found.reshape(8, 32, 128)

    ones = lanes.astype(jnp.bfloat16)
    for g in range(5):
        hits[pl.ds(8 * g, 8)] = dot(g, ones)

    def record(t, c):
        b = lanes * observed[pl.ds(t, 1), :]
        high = b.astype(jnp.bfloat16)
        low = (b - high.astype(F32)).astype(jnp.bfloat16)
        for g in range(5):
            res[t, pl.ds(8 * g, 8)] = dot(g, high) + dot(g, low)
        return c

    lax.fori_loop(0, STEPS, record, 0)

    def clear(z, c):
        for ref in (u_a, u_b, p_a, p_b, p_p, w_a, w_b, m_x):
            ref[z] = jnp.zeros((ROWS, 128), F32)
        return c

    lax.fori_loop(0, PLANES, clear, 0)
    weights[...] = band()

    def slot_of(shot, col):
        first = aperture[shot, 0]
        block_x = (first >> 3) + ((col - (first >> 3)) & 15)
        return block_slot[((block_x >> 4) << 3) + (first & 7)]

    finish(va, va_own)

    def pick(shot, c):
        slot = slot_of(shot, d)
        picks[shot] = v_2[((slot >> 2) << 1) + (slot & 1)]
        return c

    lax.fori_loop(0, SHOTS, pick, 0)
    offer = m_b.at[half_id, :, quarter(s), :]
    vb = over_shot(lambda p: picks.at[p], offer, lambda o: vb_s.at[o], lambda o: vb_r.at[o])
    vb_own = pltpu.make_async_copy(picks.at[s], offer, own_sem.at[5, 0])
    start(vb, vb_own)
    send_adjoint(1, 8)
    send_adjoint(10, 12)

    def relayout(f, dst):
        flat = dst.reshape(PLANES * ROWS, 128)

        def body(r, c):
            for g in range(4):
                flat[pl.ds((HALO + 8 * g) * ROWS + 8 + r, 8, stride=ROWS), :] = f_1[f, r, pl.ds(8 * g, 8), :]
            return c

        lax.fori_loop(0, 32, body, 0)

    def halo(src, n, land_ref, send, recv):
        def ends():
            right = pltpu.make_async_remote_copy(
                src_ref=src.at[pl.ds(HALO + 32 - n, n), pl.ds(8, 32), :],
                dst_ref=land_ref.at[0],
                send_sem=send.at[0],
                recv_sem=recv.at[0],
                device_id=(s, chunk_of(lax.rem(e + 1, DOM))),
                device_id_type=MESH,
            )
            left = pltpu.make_async_remote_copy(
                src_ref=src.at[pl.ds(HALO, n), pl.ds(8, 32), :],
                dst_ref=land_ref.at[1],
                send_sem=send.at[1],
                recv_sem=recv.at[1],
                device_id=(s, chunk_of(lax.rem(e + DOM - 1, DOM))),
                device_id_type=MESH,
            )
            return right, left

        def begin():
            right, left = ends()
            pl.when(e < DOM - 1)(right.start)
            pl.when(e > 0)(left.start)

        def sent():
            right, left = ends()
            pl.when(e < DOM - 1)(right.wait_send)
            pl.when(e > 0)(left.wait_send)

        def arrived(use):
            right, left = ends()

            @pl.when(e > 0)
            def _():
                right.wait_recv()
                use(0, HALO - n)

            @pl.when(e < DOM - 1)
            def _():
                left.wait_recv()
                use(1, HALO + 32)

        return begin, sent, arrived

    def put(dst, land_ref, n):
        def use(side, at):
            def body(z, c):
                dst[at + z, pl.ds(8, 32), :] = land_ref[side, z]
                return c

            lax.fori_loop(0, n, body, 0)

        return use

    def u_halo(par):
        return halo(u_a, 8, land.at[par], h_s.at[par], h_r.at[par])

    finish(fields[0], fields_own[0])
    relayout(0, u_a)
    u_halo(0)[0]()
    finish(fields[1], fields_own[1])
    relayout(1, u_b)
    prev_halo = halo(u_b, 4, land_p.at[0], hp_s.at[0], hp_r.at[0])
    prev_halo[0]()

    finish(vb, vb_own)
    in_first = (jnp.full((128, 128), slot_of(s, d), jnp.int32) & 2) == 0

    def choose(q, c):
        cols = pl.ds(pl.multiple_of(q * 128, 128), 128)
        for xp in range(2):
            two = [m_b[half, pl.ds(2 * xp, 2), :, cols].reshape(128, 128) for half in range(2)]
            m_t[xp, pl.ds(q * 128, 128), :] = jnp.where(in_first, two[0], two[1]).T
        return c

    lax.fori_loop(0, 4, choose, 0)
    vc = over_dom(lambda p: m_t.at[:, z_of(p), :], m_1.at[d], lambda o: vc_s.at[o], lambda o: vc_r.at[o])
    vc_own = pltpu.make_async_copy(m_t.at[:, z_of(d), :], m_1.at[d], own_sem.at[6, 0])
    start(vc, vc_own)

    send_adjoint(12, 14)
    prev_halo[2](put(u_b, land_p.at[0], 4))
    prev_halo[1]()
    finish(vc, vc_own)
    m_flat = m_x.reshape(PLANES * ROWS, 128)
    base_x = aperture[s, 0] >> 3

    def place(k, c):
        slab = m_1[(base_x + k) & 15]
        for xp in range(2):
            for g in range(4):
                m_flat[pl.ds((HALO + 8 * g) * ROWS + 8 + xp + 2 * k, 8, stride=ROWS), :] = slab[xp, 8 * g : 8 * g + 8]
        return c

    lax.fori_loop(0, 16, place, 0)
    model_halo = halo(m_x, 8, land_m, hm_s, hm_r)
    model_halo[0]()

    source = src_pos[0]
    src_z = (source & 511) - 32 * e + HALO
    src_cell = ((source >> 16) << 7) + (((source >> 15) & 1) << 6) + ((source >> 9) & 63)
    cell = (lax.broadcasted_iota(jnp.int32, (8, 128), 0) << 7) + lax.broadcasted_iota(jnp.int32, (8, 128), 1)
    steps = jnp.full((8, 128), count[0], jnp.int32)

    def tile(i):
        return pl.ds(8 + 8 * i, 8)

    def inner(i):
        return pl.ds(8 * i, 8)

    def blocks(body, first, stride, n):
        def one(j, c):
            body(first + stride * j)
            return c

        lax.fori_loop(0, n, one, 0)

    def forward(src, dst, t):
        def body(z0):
            active = steps > t
            found = []
            for z, i, mid, lap in stencil(src, z0, weights[...]):
                amount = jnp.where(z == src_z, wavelet[t], 0.0)
                u = 2.0 * mid - dst[z, tile(i), :] + m_x[z, tile(i), :] * lap
                u = u + jnp.where(cell + 1024 * i == src_cell, amount, 0.0)
                miss = jnp.where(active, hits[z - 4, inner(i), :] * u - res[t, z - 4, inner(i), :], 0.0)
                found.append((z, i, lap, u, miss))
            for z, i, lap, u, miss in found:
                laps[t, z - 4, inner(i), :] = lap
                dst[z, tile(i), :] = u
                res[t, z - 4, inner(i), :] = miss

        return body

    def fwd_pair(i, c):
        par, then = lax.rem(i, 2), lax.rem(i + 1, 2)
        step = forward(u_a, u_b, 2 * i)
        blocks(step, 12, 8, 3)

        @pl.when(i == 0)
        def _():
            model_halo[2](put(m_x, land_m, 8))
            model_halo[1]()

        u_halo(par)[2](put(u_a, land.at[par], 8))
        blocks(step, 4, 32, 2)
        u_halo(par)[1]()
        step = forward(u_b, u_a, 2 * i + 1)
        blocks(step, 8, 24, 2)

        pl.when(i < STEPS // 2 - 1)(u_halo(then)[0])
        pl.when(i == 0)(functools.partial(send_adjoint, 14, 16))

        blocks(step, 16, 8, 2)
        return c

    lax.fori_loop(0, STEPS // 2, fwd_pair, 0)
    finish(fields[2], fields_own[2])
    relayout(2, p_a)

    def p_halo(par):
        return halo(p_a, 8, land.at[par], h_s.at[par], h_r.at[par])

    def first(z, c):
        active = steps > STEPS - 1
        found = []
        for i in range(4):
            hit = p_a[z, tile(i), :] + res[STEPS - 1, z - 4, inner(i), :]
            part = jnp.where(active, hit * laps[STEPS - 1, z - 4, inner(i), :], 0.0)
            found.append((i, hit, m_x[z, tile(i), :] * hit, part))
        for i, hit, w, part in found:
            p_a[z, tile(i), :] = hit
            w_a[z, tile(i), :] = w
            grad[z - 4, inner(i), :] = part
        return c

    lax.fori_loop(8, 16, first, 0)
    lax.fori_loop(32, 40, first, 0)
    p_halo(0)[0]()
    finish(fields[3], fields_own[3])
    relayout(3, p_p)
    adj_prev_halo = halo(p_p, 4, land_p.at[1], hp_s.at[1], hp_r.at[1])
    adj_prev_halo[0]()
    lax.fori_loop(16, 32, first, 0)

    def clear_ends(z, c):
        grad[z] = jnp.zeros((32, 128), F32)
        grad[36 + z] = jnp.zeros((32, 128), F32)
        return c

    lax.fori_loop(0, 4, clear_ends, 0)

    def backward(src, dst, p_now, p_then, t):
        def body(z0):
            active, then = steps > t, steps > t - 1
            found = []
            for z, i, _, lap in stencil(src, z0, weights[...]):
                hit = p_now[z, tile(i), :]
                prev = p_p[z, tile(i), :]
                cur = jnp.where(active, 2.0 * hit - prev + lap, hit)
                prev = jnp.where(active, hit, prev)
                hit = cur + res[t - 1, z - 4, inner(i), :]
                part = jnp.where(then, hit * laps[t - 1, z - 4, inner(i), :], 0.0)
                found.append((z, i, prev, hit, m_x[z, tile(i), :] * hit, grad[z - 4, inner(i), :] + part))
            for z, i, prev, hit, w, total in found:
                p_p[z, tile(i), :] = prev
                p_then[z, tile(i), :] = hit
                dst[z, tile(i), :] = w
                grad[z - 4, inner(i), :] = total

        return body

    def adj_ends(land_ref, t):
        stepped = steps > t + 1

        def use(side, at):
            near = at + 4 * (1 - side)

            def keep(z, c):
                for i in range(4):
                    p_p[z, tile(i), :] = jnp.where(stepped, p_b[z, tile(i), :], p_p[z, tile(i), :])
                return c

            lax.fori_loop(near, near + 4, keep, 0)

            def body(z, c):
                hit = land_ref[side, z]
                p_a[at + z, pl.ds(8, 32), :] = hit
                w_a[at + z, pl.ds(8, 32), :] = m_x[at + z, pl.ds(8, 32), :] * hit
                return c

            lax.fori_loop(0, 8, body, 0)

        return use

    def adj_pair(i, c):
        par, then = lax.rem(i, 2), lax.rem(i + 1, 2)
        t = STEPS - 1 - 2 * i
        step = backward(w_a, w_b, p_a, p_b, t)
        pl.when(i == 0)(adj_prev_halo[1])
        blocks(step, 12, 8, 3)

        @pl.when(i == 0)
        def _():
            adj_prev_halo[2](put(p_p, land_p.at[1], 4))

        p_halo(par)[2](adj_ends(land.at[par], t))
        blocks(step, 4, 32, 2)
        p_halo(par)[1]()

        @pl.when(i < STEPS // 2 - 1)
        def _():
            step = backward(w_b, w_a, p_b, p_a, t - 1)
            blocks(step, 8, 24, 2)
            p_halo(then)[0]()
            blocks(step, 16, 8, 2)

        return c

    lax.fori_loop(0, STEPS // 2, adj_pair, 0)

    g_flat = grad.reshape(40 * 32, 128)

    gd, gd_own = [], []
    for h in range(2):

        def gather(k, c, h=h):
            for g in range(4):
                g_1[h, k, pl.ds(8 * g, 8), :] = g_flat[pl.ds((4 + 8 * g) * 32 + h + 2 * k, 8, stride=32), :]
            return c

        lax.fori_loop(0, 16, gather, 0)

        def turn(col, c, h=h):
            g_send[h, col] = g_1[h, (col - base_x) & 15]
            return c

        lax.fori_loop(0, 16, turn, 0)
        gd.append(
            over_dom(
                lambda p, h=h: g_send.at[h, p],
                g_t.at[h, z_of(d), :],
                lambda o, h=h: gd_s.at[h, o],
                lambda o, h=h: gd_r.at[h, o],
            )
        )
        gd_own.append(pltpu.make_async_copy(g_send.at[h, d], g_t.at[h, z_of(d), :], own_sem.at[7, h]))
        start(gd[h], gd_own[h])

    gf, gf_own = [], []
    for h in range(2):
        finish(gd[h], gd_own[h])
        half = pl.ds(2 * h, 2)

        def back(q, c, h=h, half=half):
            cols = pl.ds(pl.multiple_of(q * 128, 128), 128)
            g_b[half, :, cols] = g_t[h, pl.ds(q * 128, 128), :].T.reshape(2, 64, 128)
            return c

        lax.fori_loop(0, 4, back, 0)
        gf.append(
            over_shot(
                lambda p, half=half: g_b.at[half, rows_of(p), :],
                g_recv.at[h, s],
                lambda o, h=h: gf_s.at[h, o],
                lambda o, h=h: gf_r.at[h, o],
            )
        )
        gf_own.append(pltpu.make_async_copy(g_b.at[half, rows_of(s), :], g_recv.at[h, s], own_sem.at[8, h]))
        start(gf[h], gf_own[h])

    owners = [jnp.full((8, 128), slot_of(shot, d), jnp.int32) for shot in range(SHOTS)]
    gg, gg_own = [], []
    for h in range(2):
        finish(gf[h], gf_own[h])
        half = pl.ds(2 * h, 2)

        def add_up(slot, c, h=h):
            mine = [owner == slot for owner in owners]
            sums = []
            for x in range(2):
                for q in range(4):
                    total = jnp.zeros((8, 128), F32)
                    for shot in range(SHOTS):
                        total = total + jnp.where(mine[shot], g_recv[h, shot, x, :, pl.ds(128 * q, 128)], 0.0)
                    sums.append((x, q, total))
            for x, q, total in sums:
                batch[h, slot, x, :, pl.ds(128 * q, 128)] = total
            return c

        lax.fori_loop(0, 16, add_up, 0)
        target = out.at[:, half, rows_of(s), :]
        gg.append(
            over_shot(
                lambda p, h=h: batch.at[h, pl.ds(2 * p, 2)],
                target,
                lambda o, h=h: gg_s.at[h, o],
                lambda o, h=h: gg_r.at[h, o],
            )
        )
        gg_own.append(pltpu.make_async_copy(batch.at[h, pl.ds(2 * s, 2)], target, own_sem.at[9, h]))
        start(gg[h], gg_own[h])
    for h in range(2):
        finish(gg[h], gg_own[h])


def local(
    velocity,
    fwd_prev,
    fwd_cur,
    adj_prev,
    adj_cur,
    wavelet,
    src_pos,
    rec_pos,
    observed,
    step_count,
    aperture,
    block_slot,
    prev_batch,
    snapshot,
):
    shape = (2, 4, 64, 512)
    hbm = pl.BlockSpec(memory_space=pl.ANY)
    vmem = pl.BlockSpec(memory_space=pltpu.VMEM)
    smem = pl.BlockSpec(memory_space=pltpu.SMEM)
    field = pltpu.VMEM((PLANES, ROWS, 128), F32)
    dma = pltpu.SemaphoreType.DMA
    scratch = [
        pltpu.VMEM((8, 4, 16, 512), F32),
        pltpu.VMEM((8, 4, 16, 512), F32),
        pltpu.VMEM((2, 4, 64, 512), F32),
        pltpu.VMEM((2, 512, 128), F32),
        pltpu.VMEM((16, 2, 32, 128), F32),
        pltpu.VMEM((4, 4, 64, 512), F32),
        pltpu.VMEM((4, 2, 512, 128), F32),
        pltpu.VMEM((4, 32, 32, 128), F32),
        *[field] * 8,
        pltpu.VMEM((STEPS, 40, 32, 128), F32),
        pltpu.VMEM((STEPS, 40, 32, 128), F32),
        pltpu.VMEM((40, 32, 128), F32),
        pltpu.VMEM((5, 256, 256), jnp.bfloat16),
        pltpu.VMEM((256, 256), jnp.bfloat16),
        pltpu.VMEM((40, 32, 128), F32),
        pltpu.VMEM((2, 2, 8, 32, 128), F32),
        pltpu.VMEM((2, 8, 32, 128), F32),
        pltpu.VMEM((2, 2, 4, 32, 128), F32),
        pltpu.VMEM((2, 16, 32, 128), F32),
        pltpu.VMEM((2, 16, 32, 128), F32),
        pltpu.VMEM((2, 512, 128), F32),
        pltpu.VMEM((4, 64, 512), F32),
        pltpu.VMEM((2, 8, 2, 8, 512), F32),
        pltpu.VMEM((2, 16, 2, 8, 512), F32),
        dma((4,)),
        dma((10, 2)),
        dma((4,)), dma((4,)),
        dma((4, 16)), dma((4, 16)),
        dma((8,)), dma((8,)),
        dma((16,)), dma((16,)),
        dma((2, 16)), dma((2, 16)),
        dma((2, 8)), dma((2, 8)),
        dma((2, 8)), dma((2, 8)),
        dma((2, 2)), dma((2, 2)),
        dma((2,)), dma((2,)),
        dma((2, 2)), dma((2, 2)),
    ]
    batch = pl.pallas_call(
        kernel,
        out_shape=jax.ShapeDtypeStruct(shape, F32),
        in_specs=[hbm] * 5 + [vmem] * 2 + [smem] * 5,
        out_specs=hbm,
        scratch_shapes=scratch,
        name="adjoint_gradient",
        compiler_params=pltpu.CompilerParams(collective_id=0, has_side_effects=True, vmem_limit_bytes=56 << 20),
    )(
        velocity.reshape(shape),
        fwd_cur[0],
        fwd_prev[0],
        adj_cur[0],
        adj_prev[0],
        rec_pos,
        observed[0],
        wavelet[0],
        src_pos,
        step_count,
        aperture,
        block_slot,
    )
    result = (batch - prev_batch.reshape(shape)) + snapshot.reshape(shape)
    return result.reshape(velocity.shape)


def solution(mesh):
    placed = (
        P("shot", "dom", None, None, None),
        P("shot", "dom", None, None),
        P("shot", "dom", None, None),
        P("shot", "dom", None, None),
        P("shot", "dom", None, None),
        P("shot", None),
        P("shot"),
        P("shot", None),
        P("shot", None, None),
        P("shot"),
        P(),
        P(),
        P("shot", "dom", None, None, None),
        P("shot", "dom", None, None, None),
    )
    return jax.shard_map(
        local,
        mesh=mesh,
        in_specs=placed,
        out_specs=P("shot", "dom", None, None, None),
        check_vma=False,
    )
```

```python
import functools

import jax
import jax.numpy as jnp
from jax import lax
from jax.experimental import pallas as pl
from jax.experimental.pallas import tpu as pltpu
from jax.sharding import PartitionSpec as P

C0, C1, C2, C3, C4 = (-205.0 / 72.0, 8.0 / 5.0, -1.0 / 5.0, 8.0 / 315.0, -1.0 / 560.0)
MESH = pl.DeviceIdType.MESH
F32 = jnp.float32
SHOTS, DOM, STEPS = 8, 16, 8
HALO = 8
PLANES, ROWS = 48, 48


def chunk_of(d):
    return d + (d // 8) * (23 - 2 * d)


def band():
    row = lax.broadcasted_iota(jnp.int32, (256, 256), 0)
    col = lax.broadcasted_iota(jnp.int32, (256, 256), 1)
    gap = jnp.abs((row & 127) - (col & 127))
    same = ((row >> 6) & 1) == ((col >> 6) & 1)
    full = jnp.where(same & (gap == 0), 3.0 * C0, 0.0)
    for k, c in ((1, C1), (2, C2), (3, C3), (4, C4)):
        full = full + jnp.where(same & (gap == k), c, 0.0)
    high = full.astype(jnp.bfloat16).astype(F32)
    low = jnp.where(row < 128, full - high, 0.0)
    return jnp.where(col < 128, high, low).astype(jnp.bfloat16)


def stencil(ref, z0, weights):
    low = lax.broadcasted_iota(jnp.int32, (8, 128), 1) < 64
    cells = jnp.concatenate([ref[z0 + p, pl.ds(8, 32), :] for p in range(8)], 0)
    high = cells.astype(jnp.bfloat16)
    rest = (cells - high.astype(F32)).astype(jnp.bfloat16)
    along_y = jnp.dot(jnp.concatenate([high, rest], 1), weights, preferred_element_type=F32)
    along_y = along_y[:, :128] + along_y[:, 128:]
    for p in range(8):
        z = z0 + p
        for i in range(4):
            row = 8 + 8 * i
            mid = ref[z, pl.ds(row, 8), :]
            pairs = [ref[z + k, pl.ds(row, 8), :] + ref[z - k, pl.ds(row, 8), :] for k in (1, 2, 3, 4)]
            up1, up2, dn1, dn2 = (ref[z, pl.ds(row + k, 8), :] for k in (1, 2, -1, -2))
            pairs[1] = pairs[1] + (up1 + dn1)
            pairs[3] = pairs[3] + (up2 + dn2)
            odd = C1 * (jnp.where(low, up1, mid) + jnp.where(low, mid, dn1))
            odd = odd + C3 * (jnp.where(low, up2, up1) + jnp.where(low, dn1, dn2))
            total = C1 * pairs[0] + C2 * pairs[1] + C3 * pairs[2] + C4 * pairs[3]
            lap = total + pltpu.roll(odd, 64, 1) + along_y[32 * p + 8 * i : 32 * p + 8 * i + 8]
            yield z, i, mid, lap


def kernel(
    vel, fwd_cur, fwd_prev, adj_cur, adj_prev, rec_pos, observed, wavelet, src_pos, count, aperture, block_slot,
    out,
    v_2a, v_2b, picks, m_b, m_t, m_1, f_in, f_t, f_1,
    u_a, u_b, p_a, p_b, p_p, w_a, w_b, m_x, laps, res, hits, onehot, weights, grad, land, land_m, land_p,
    g_1, g_send, g_t, g_b, g_recv, batch,
    in_sem, own_sem, va_s, va_r, f_s, f_r, vb_s, vb_r, vc_s, vc_r, gd_s, gd_r, gf_s, gf_r, gg_s, gg_r,
    h_s, h_r, hm_s, hm_r, hp_s, hp_r,
):
    s, d = lax.axis_index("shot"), lax.axis_index("dom")
    e = chunk_of(d)
    x, half_id = s // 2, lax.rem(s, 2)

    loads = []
    for f, ref in enumerate((fwd_cur, fwd_prev, adj_cur, adj_prev)):
        loads.append(pltpu.make_async_copy(ref, f_in.at[f], in_sem.at[f]))
        loads[-1].start()

    barrier = pltpu.get_barrier_semaphore()
    for o in range(1, DOM):
        pl.semaphore_signal(barrier, inc=1, device_id=(s, lax.rem(d + o, DOM)), device_id_type=MESH)
    for o in range(1, SHOTS):
        pl.semaphore_signal(barrier, inc=1, device_id=(lax.rem(s + o, SHOTS), d), device_id_type=MESH)

    def partner(o):
        return lax.rem(d // 8 + o // 8, 2) * 8 + lax.rem(d + o, 8)

    def over_dom(src, dst, send, recv):
        def copy(o):
            p = partner(o)
            return pltpu.make_async_remote_copy(
                src_ref=src(p), dst_ref=dst, send_sem=send(o), recv_sem=recv(o), device_id=(s, p), device_id_type=MESH
            )

        return copy, DOM

    def over_shot(src, dst, send, recv):
        def copy(o):
            p = lax.rem(s + o, SHOTS)
            return pltpu.make_async_remote_copy(
                src_ref=src(p), dst_ref=dst, send_sem=send(o), recv_sem=recv(o), device_id=(p, d), device_id_type=MESH
            )

        return copy, SHOTS

    def over_x(src, dst, send, recv):
        def copy(o):
            p = lax.rem(s + 2 * o, SHOTS)
            return pltpu.make_async_remote_copy(
                src_ref=src(p), dst_ref=dst, send_sem=send(o), recv_sem=recv(o), device_id=(p, d), device_id_type=MESH
            )

        return copy, SHOTS // 2

    def start(exchange, own):
        copy, n = exchange

        def body(k, c):
            copy(2 * k - 1 - 7 * (k // 5) if n == SHOTS else n - k).start()
            return c

        lax.fori_loop(1, n, body, 0, unroll=True)
        own.start()

    def finish(exchange, own):
        copy, n = exchange

        def body(o, c):
            copy(o).wait()
            return c

        lax.fori_loop(1, n, body, 0, unroll=True)
        own.wait()

    def transpose_pair(src, dst, xp):
        def body(q, c):
            block = src[pl.ds(2 * xp, 2), :, pl.ds(pl.multiple_of(q * 128, 128), 128)]
            dst[xp, pl.ds(q * 128, 128), :] = block.reshape(128, 128).T
            return c

        lax.fori_loop(0, 4, body, 0)

    def transpose_in(src, dst):
        for xp in range(2):
            transpose_pair(src, dst, xp)

    def z_of(p):
        return pl.ds(chunk_of(p) * 32, 32)

    def rows_of(p):
        return pl.ds(p * 8, 8)

    def quarter(p):
        return pl.ds((p // 2) * 16, 16)

    loads[0].wait()
    transpose_in(f_in.at[0], f_t.at[0])
    pl.semaphore_wait(barrier, DOM + SHOTS - 2)
    va, va_own = [], []
    for h in range(2):
        half = pl.ds(2 * h, 2)
        mine = (v_2a, v_2b)[h].at[pl.ds(2 * x, 2)]
        va.append(
            over_x(
                lambda p, half=half: vel.at[:, half, quarter(p), :],
                mine,
                lambda o, h=h: va_s.at[h, o],
                lambda o, h=h: va_r.at[h, o],
            )
        )
        va_own.append(pltpu.make_async_copy(vel.at[:, half, quarter(s), :], mine, own_sem.at[0, h]))
        start(va[h], va_own[h])

    fields, fields_own = [], []
    for f in range(4):
        fields.append(
            over_dom(
                lambda p, f=f: f_t.at[f, :, z_of(p), :],
                f_1.at[f, pl.ds(2 * d, 2)],
                lambda o, f=f: f_s.at[f, o],
                lambda o, f=f: f_r.at[f, o],
            )
        )
        fields_own.append(pltpu.make_async_copy(f_t.at[f, :, z_of(d), :], f_1.at[f, pl.ds(2 * d, 2)], own_sem.at[1 + f, 0]))
    start(fields[0], fields_own[0])
    loads[1].wait()
    transpose_in(f_in.at[1], f_t.at[1])
    start(fields[1], fields_own[1])
    for f in range(2, 4):
        loads[f].wait()
        transpose_in(f_in.at[f], f_t.at[f])

    def send_adjoint(lo, hi):
        for f in range(2, 4):

            def body(o, c, f=f):
                fields[f][0](o).start()
                return c

            lax.fori_loop(lo, hi, body, 0)

    for f in range(2, 4):
        fields_own[f].start()

    pos = rec_pos[...]
    rec_row = (((pos & 511) - 32 * e + 4) << 5) + (pos >> 16)
    rec_lane = (((pos >> 15) & 1) << 6) + ((pos >> 9) & 63)
    row_id = lax.broadcasted_iota(jnp.int32, (256, 256), 0)
    for g in range(5):
        onehot[g] = (row_id + 256 * g == rec_row).astype(F32).astype(jnp.bfloat16)
    lanes = (lax.broadcasted_iota(jnp.int32, (128, 256), 0) == rec_lane).astype(F32)

    def dot(g, b):
        found = lax.dot_general(onehot[g], b, (((1,), (1,)), ((), ())), preferred_element_type=F32)
        return found.reshape(8, 32, 128)

    ones = lanes.astype(jnp.bfloat16)
    for g in range(5):
        hits[pl.ds(8 * g, 8)] = dot(g, ones)

    def record(t, c):
        b = lanes * observed[pl.ds(t, 1), :]
        high = b.astype(jnp.bfloat16)
        low = (b - high.astype(F32)).astype(jnp.bfloat16)
        for g in range(5):
            res[t, pl.ds(8 * g, 8)] = dot(g, high) + dot(g, low)
        return c

    lax.fori_loop(0, STEPS, record, 0)

    def clear(z, c):
        for ref in (u_a, u_b, p_a, p_b, p_p, w_a, w_b, m_x):
            ref[z] = jnp.zeros((ROWS, 128), F32)
        return c

    lax.fori_loop(0, PLANES, clear, 0)
    weights[...] = band()

    def slot_of(shot, col):
        first = aperture[shot, 0]
        block_x = (first >> 3) + ((col - (first >> 3)) & 15)
        return block_slot[((block_x >> 4) << 3) + (first & 7)]

    vb, vb_own = [], []
    for h in range(2):
        finish(va[h], va_own[h])

        def pick(shot, c, h=h):
            slot = slot_of(shot, d)
            picks[h, shot] = (v_2a, v_2b)[h][((slot >> 2) << 1) + (slot & 1)]
            return c

        lax.fori_loop(0, SHOTS, pick, 0)
        offer = m_b.at[half_id, pl.ds(2 * h, 2), quarter(s), :]
        vb.append(
            over_shot(lambda p, h=h: picks.at[h, p], offer, lambda o, h=h: vb_s.at[h, o], lambda o, h=h: vb_r.at[h, o])
        )
        vb_own.append(pltpu.make_async_copy(picks.at[h, s], offer, own_sem.at[5, h]))
        start(vb[h], vb_own[h])
    send_adjoint(1, 8)

    def relayout(f, dst):
        flat = dst.reshape(PLANES * ROWS, 128)

        def body(r, c):
            for g in range(4):
                flat[pl.ds((HALO + 8 * g) * ROWS + 8 + r, 8, stride=ROWS), :] = f_1[f, r, pl.ds(8 * g, 8), :]
            return c

        lax.fori_loop(0, 32, body, 0)

    def halo(src, n, land_ref, send, recv):
        def ends():
            right = pltpu.make_async_remote_copy(
                src_ref=src.at[pl.ds(HALO + 32 - n, n), pl.ds(8, 32), :],
                dst_ref=land_ref.at[0],
                send_sem=send.at[0],
                recv_sem=recv.at[0],
                device_id=(s, chunk_of(lax.rem(e + 1, DOM))),
                device_id_type=MESH,
            )
            left = pltpu.make_async_remote_copy(
                src_ref=src.at[pl.ds(HALO, n), pl.ds(8, 32), :],
                dst_ref=land_ref.at[1],
                send_sem=send.at[1],
                recv_sem=recv.at[1],
                device_id=(s, chunk_of(lax.rem(e + DOM - 1, DOM))),
                device_id_type=MESH,
            )
            return right, left

        def begin():
            right, left = ends()
            pl.when(e < DOM - 1)(right.start)
            pl.when(e > 0)(left.start)

        def sent():
            right, left = ends()
            pl.when(e < DOM - 1)(right.wait_send)
            pl.when(e > 0)(left.wait_send)

        def arrived(use):
            right, left = ends()

            @pl.when(e > 0)
            def _():
                right.wait_recv()
                use(0, HALO - n)

            @pl.when(e < DOM - 1)
            def _():
                left.wait_recv()
                use(1, HALO + 32)

        return begin, sent, arrived

    def put(dst, land_ref, n):
        def use(side, at):
            def body(z, c):
                dst[at + z, pl.ds(8, 32), :] = land_ref[side, z]
                return c

            lax.fori_loop(0, n, body, 0)

        return use

    def u_halo(par):
        return halo(u_a, 8, land.at[par], h_s.at[par], h_r.at[par])

    finish(fields[0], fields_own[0])
    relayout(0, u_a)
    u_halo(0)[0]()
    finish(fields[1], fields_own[1])
    relayout(1, u_b)
    prev_halo = halo(u_b, 4, land_p.at[0], hp_s.at[0], hp_r.at[0])
    prev_halo[0]()

    in_first = (jnp.full((128, 128), slot_of(s, d), jnp.int32) & 2) == 0
    vc, vc_own = [], []
    for h in range(2):
        finish(vb[h], vb_own[h])

        def choose(q, c, h=h):
            cols = pl.ds(pl.multiple_of(q * 128, 128), 128)
            two = [m_b[part, pl.ds(2 * h, 2), :, cols].reshape(128, 128) for part in range(2)]
            m_t[h, pl.ds(q * 128, 128), :] = jnp.where(in_first, two[0], two[1]).T
            return c

        lax.fori_loop(0, 4, choose, 0)
        vc.append(
            over_dom(
                lambda p, h=h: m_t.at[h, z_of(p), :],
                m_1.at[d, h],
                lambda o, h=h: vc_s.at[h, o],
                lambda o, h=h: vc_r.at[h, o],
            )
        )
        vc_own.append(pltpu.make_async_copy(m_t.at[h, z_of(d), :], m_1.at[d, h], own_sem.at[6, h]))
        start(vc[h], vc_own[h])
    send_adjoint(8, 10)
    prev_halo[2](put(u_b, land_p.at[0], 4))
    prev_halo[1]()
    for h in range(2):
        finish(vc[h], vc_own[h])
    m_flat = m_x.reshape(PLANES * ROWS, 128)
    base_x = aperture[s, 0] >> 3

    def place(k, c):
        slab = m_1[(base_x + k) & 15]
        for xp in range(2):
            for g in range(4):
                m_flat[pl.ds((HALO + 8 * g) * ROWS + 8 + xp + 2 * k, 8, stride=ROWS), :] = slab[xp, 8 * g : 8 * g + 8]
        return c

    lax.fori_loop(0, 16, place, 0)
    model_halo = halo(m_x, 8, land_m, hm_s, hm_r)
    model_halo[0]()

    source = src_pos[0]
    src_z = (source & 511) - 32 * e + HALO
    src_cell = ((source >> 16) << 7) + (((source >> 15) & 1) << 6) + ((source >> 9) & 63)
    cell = (lax.broadcasted_iota(jnp.int32, (8, 128), 0) << 7) + lax.broadcasted_iota(jnp.int32, (8, 128), 1)
    steps = jnp.full((8, 128), count[0], jnp.int32)

    def tile(i):
        return pl.ds(8 + 8 * i, 8)

    def inner(i):
        return pl.ds(8 * i, 8)

    def blocks(body, first, stride, n):
        def one(j, c):
            body(first + stride * j)
            return c

        lax.fori_loop(0, n, one, 0)

    def forward(src, dst, t):
        def body(z0):
            active = steps > t
            found = []
            for z, i, mid, lap in stencil(src, z0, weights[...]):
                amount = jnp.where(z == src_z, wavelet[t], 0.0)
                u = 2.0 * mid - dst[z, tile(i), :] + m_x[z, tile(i), :] * lap
                u = u + jnp.where(cell + 1024 * i == src_cell, amount, 0.0)
                miss = jnp.where(active, hits[z - 4, inner(i), :] * u - res[t, z - 4, inner(i), :], 0.0)
                found.append((z, i, lap, u, miss))
            for z, i, lap, u, miss in found:
                laps[t, z - 4, inner(i), :] = lap
                dst[z, tile(i), :] = u
                res[t, z - 4, inner(i), :] = miss

        return body

    def fwd_pair(i, c):
        par, then = lax.rem(i, 2), lax.rem(i + 1, 2)
        step = forward(u_a, u_b, 2 * i)
        blocks(step, 12, 8, 3)

        @pl.when(i == 0)
        def _():
            model_halo[2](put(m_x, land_m, 8))
            model_halo[1]()

        @pl.when(i == STEPS // 2 - 1)
        def _():
            for f, dst in ((2, p_a), (3, p_p)):
                finish(fields[f], fields_own[f])
                relayout(f, dst)

        u_halo(par)[2](put(u_a, land.at[par], 8))
        blocks(step, 4, 32, 2)
        u_halo(par)[1]()
        step = forward(u_b, u_a, 2 * i + 1)
        blocks(step, 8, 24, 2)


        @pl.when(i < STEPS // 2 - 1)
        def _():
            u_halo(then)[0]()
            send_adjoint(10 + 2 * i, 12 + 2 * i)

        blocks(step, 16, 8, 2)
        return c

    lax.fori_loop(0, STEPS // 2, fwd_pair, 0)

    def p_halo(par):
        return halo(p_a, 8, land.at[par], h_s.at[par], h_r.at[par])

    def first(z, c):
        active = steps > STEPS - 1
        found = []
        for i in range(4):
            hit = p_a[z, tile(i), :] + res[STEPS - 1, z - 4, inner(i), :]
            part = jnp.where(active, hit * laps[STEPS - 1, z - 4, inner(i), :], 0.0)
            found.append((i, hit, m_x[z, tile(i), :] * hit, part))
        for i, hit, w, part in found:
            p_a[z, tile(i), :] = hit
            w_a[z, tile(i), :] = w
            grad[z - 4, inner(i), :] = part
        return c

    lax.fori_loop(8, 16, first, 0)
    lax.fori_loop(32, 40, first, 0)
    p_halo(0)[0]()
    adj_prev_halo = halo(p_p, 4, land_p.at[1], hp_s.at[1], hp_r.at[1])
    adj_prev_halo[0]()
    lax.fori_loop(16, 32, first, 0)

    def clear_ends(z, c):
        grad[z] = jnp.zeros((32, 128), F32)
        grad[36 + z] = jnp.zeros((32, 128), F32)
        return c

    lax.fori_loop(0, 4, clear_ends, 0)

    def backward(src, dst, p_now, p_then, t):
        def body(z0):
            active, then = steps > t, steps > t - 1
            found = []
            for z, i, _, lap in stencil(src, z0, weights[...]):
                hit = p_now[z, tile(i), :]
                prev = p_p[z, tile(i), :]
                cur = jnp.where(active, 2.0 * hit - prev + lap, hit)
                prev = jnp.where(active, hit, prev)
                hit = cur + res[t - 1, z - 4, inner(i), :]
                part = jnp.where(then, hit * laps[t - 1, z - 4, inner(i), :], 0.0)
                found.append((z, i, prev, hit, m_x[z, tile(i), :] * hit, grad[z - 4, inner(i), :] + part))
            for z, i, prev, hit, w, total in found:
                p_p[z, tile(i), :] = prev
                p_then[z, tile(i), :] = hit
                dst[z, tile(i), :] = w
                grad[z - 4, inner(i), :] = total

        return body

    def adj_ends(land_ref, t):
        stepped = steps > t + 1

        def use(side, at):
            near = at + 4 * (1 - side)

            def keep(z, c):
                for i in range(4):
                    p_p[z, tile(i), :] = jnp.where(stepped, p_b[z, tile(i), :], p_p[z, tile(i), :])
                return c

            lax.fori_loop(near, near + 4, keep, 0)

            def body(z, c):
                hit = land_ref[side, z]
                p_a[at + z, pl.ds(8, 32), :] = hit
                w_a[at + z, pl.ds(8, 32), :] = m_x[at + z, pl.ds(8, 32), :] * hit
                return c

            lax.fori_loop(0, 8, body, 0)

        return use

    def adj_pair(i, c):
        par, then = lax.rem(i, 2), lax.rem(i + 1, 2)
        t = STEPS - 1 - 2 * i
        step = backward(w_a, w_b, p_a, p_b, t)
        pl.when(i == 0)(adj_prev_halo[1])
        blocks(step, 12, 8, 3)

        @pl.when(i == 0)
        def _():
            adj_prev_halo[2](put(p_p, land_p.at[1], 4))

        p_halo(par)[2](adj_ends(land.at[par], t))
        blocks(step, 4, 32, 2)
        p_halo(par)[1]()

        @pl.when(i < STEPS // 2 - 1)
        def _():
            step = backward(w_b, w_a, p_b, p_a, t - 1)
            blocks(step, 8, 24, 2)
            p_halo(then)[0]()
            blocks(step, 16, 8, 2)

        return c

    lax.fori_loop(0, STEPS // 2, adj_pair, 0)

    g_flat = grad.reshape(40 * 32, 128)

    gd, gd_own = [], []
    for h in range(2):

        def gather(k, c, h=h):
            for g in range(4):
                g_1[h, k, pl.ds(8 * g, 8), :] = g_flat[pl.ds((4 + 8 * g) * 32 + h + 2 * k, 8, stride=32), :]
            return c

        lax.fori_loop(0, 16, gather, 0)

        def turn(col, c, h=h):
            g_send[h, col] = g_1[h, (col - base_x) & 15]
            return c

        lax.fori_loop(0, 16, turn, 0)
        gd.append(
            over_dom(
                lambda p, h=h: g_send.at[h, p],
                g_t.at[h, z_of(d), :],
                lambda o, h=h: gd_s.at[h, o],
                lambda o, h=h: gd_r.at[h, o],
            )
        )
        gd_own.append(pltpu.make_async_copy(g_send.at[h, d], g_t.at[h, z_of(d), :], own_sem.at[7, h]))
        start(gd[h], gd_own[h])

    gf, gf_own = [], []
    for h in range(2):
        finish(gd[h], gd_own[h])
        half = pl.ds(2 * h, 2)

        def back(q, c, h=h, half=half):
            cols = pl.ds(pl.multiple_of(q * 128, 128), 128)
            g_b[half, :, cols] = g_t[h, pl.ds(q * 128, 128), :].T.reshape(2, 64, 128)
            return c

        lax.fori_loop(0, 4, back, 0)
        gf.append(
            over_shot(
                lambda p, half=half: g_b.at[half, rows_of(p), :],
                g_recv.at[h, s],
                lambda o, h=h: gf_s.at[h, o],
                lambda o, h=h: gf_r.at[h, o],
            )
        )
        gf_own.append(pltpu.make_async_copy(g_b.at[half, rows_of(s), :], g_recv.at[h, s], own_sem.at[8, h]))
        start(gf[h], gf_own[h])

    owners = [jnp.full((8, 128), slot_of(shot, d), jnp.int32) for shot in range(SHOTS)]
    gg, gg_own = [], []
    for h in range(2):
        finish(gf[h], gf_own[h])
        half = pl.ds(2 * h, 2)

        def add_up(slot, c, h=h):
            mine = [owner == slot for owner in owners]
            sums = []
            for x in range(2):
                for q in range(4):
                    total = jnp.zeros((8, 128), F32)
                    for shot in range(SHOTS):
                        total = total + jnp.where(mine[shot], g_recv[h, shot, x, :, pl.ds(128 * q, 128)], 0.0)
                    sums.append((x, q, total))
            for x, q, total in sums:
                batch[h, slot, x, :, pl.ds(128 * q, 128)] = total
            return c

        lax.fori_loop(0, 16, add_up, 0)
        target = out.at[:, half, rows_of(s), :]
        gg.append(
            over_shot(
                lambda p, h=h: batch.at[h, pl.ds(2 * p, 2)],
                target,
                lambda o, h=h: gg_s.at[h, o],
                lambda o, h=h: gg_r.at[h, o],
            )
        )
        gg_own.append(pltpu.make_async_copy(batch.at[h, pl.ds(2 * s, 2)], target, own_sem.at[9, h]))
        start(gg[h], gg_own[h])
    for h in range(2):
        finish(gg[h], gg_own[h])


def local(
    velocity,
    fwd_prev,
    fwd_cur,
    adj_prev,
    adj_cur,
    wavelet,
    src_pos,
    rec_pos,
    observed,
    step_count,
    aperture,
    block_slot,
    prev_batch,
    snapshot,
):
    shape = (2, 4, 64, 512)
    hbm = pl.BlockSpec(memory_space=pl.ANY)
    vmem = pl.BlockSpec(memory_space=pltpu.VMEM)
    smem = pl.BlockSpec(memory_space=pltpu.SMEM)
    field = pltpu.VMEM((PLANES, ROWS, 128), F32)
    dma = pltpu.SemaphoreType.DMA
    scratch = [
        pltpu.VMEM((8, 2, 16, 512), F32),
        pltpu.VMEM((8, 2, 16, 512), F32),
        pltpu.VMEM((2, 8, 2, 16, 512), F32),
        pltpu.VMEM((2, 4, 64, 512), F32),
        pltpu.VMEM((2, 512, 128), F32),
        pltpu.VMEM((16, 2, 32, 128), F32),
        pltpu.VMEM((4, 4, 64, 512), F32),
        pltpu.VMEM((4, 2, 512, 128), F32),
        pltpu.VMEM((4, 32, 32, 128), F32),
        *[field] * 8,
        pltpu.VMEM((STEPS, 40, 32, 128), F32),
        pltpu.VMEM((STEPS, 40, 32, 128), F32),
        pltpu.VMEM((40, 32, 128), F32),
        pltpu.VMEM((5, 256, 256), jnp.bfloat16),
        pltpu.VMEM((256, 256), jnp.bfloat16),
        pltpu.VMEM((40, 32, 128), F32),
        pltpu.VMEM((2, 2, 8, 32, 128), F32),
        pltpu.VMEM((2, 8, 32, 128), F32),
        pltpu.VMEM((2, 2, 4, 32, 128), F32),
        pltpu.VMEM((2, 16, 32, 128), F32),
        pltpu.VMEM((2, 16, 32, 128), F32),
        pltpu.VMEM((2, 512, 128), F32),
        pltpu.VMEM((4, 64, 512), F32),
        pltpu.VMEM((2, 8, 2, 8, 512), F32),
        pltpu.VMEM((2, 16, 2, 8, 512), F32),
        dma((4,)),
        dma((10, 2)),
        dma((2, 4)), dma((2, 4)),
        dma((4, 16)), dma((4, 16)),
        dma((2, 8)), dma((2, 8)),
        dma((2, 16)), dma((2, 16)),
        dma((2, 16)), dma((2, 16)),
        dma((2, 8)), dma((2, 8)),
        dma((2, 8)), dma((2, 8)),
        dma((2, 2)), dma((2, 2)),
        dma((2,)), dma((2,)),
        dma((2, 2)), dma((2, 2)),
    ]
    batch = pl.pallas_call(
        kernel,
        out_shape=jax.ShapeDtypeStruct(shape, F32),
        in_specs=[hbm] * 5 + [vmem] * 2 + [smem] * 5,
        out_specs=hbm,
        scratch_shapes=scratch,
        name="adjoint_gradient",
        compiler_params=pltpu.CompilerParams(collective_id=0, has_side_effects=True, vmem_limit_bytes=56 << 20),
    )(
        velocity.reshape(shape),
        fwd_cur[0],
        fwd_prev[0],
        adj_cur[0],
        adj_prev[0],
        rec_pos,
        observed[0],
        wavelet[0],
        src_pos,
        step_count,
        aperture,
        block_slot,
    )
    result = (batch - prev_batch.reshape(shape)) + snapshot.reshape(shape)
    return result.reshape(velocity.shape)


def solution(mesh):
    placed = (
        P("shot", "dom", None, None, None),
        P("shot", "dom", None, None),
        P("shot", "dom", None, None),
        P("shot", "dom", None, None),
        P("shot", "dom", None, None),
        P("shot", None),
        P("shot"),
        P("shot", None),
        P("shot", None, None),
        P("shot"),
        P(),
        P(),
        P("shot", "dom", None, None, None),
        P("shot", "dom", None, None, None),
    )
    return jax.shard_map(
        local,
        mesh=mesh,
        in_specs=placed,
        out_specs=P("shot", "dom", None, None, None),
        check_vma=False,
    )
```

```python
import functools

import jax
import jax.numpy as jnp
from jax import lax
from jax.experimental import pallas as pl
from jax.experimental.pallas import tpu as pltpu
from jax.sharding import PartitionSpec as P

C0, C1, C2, C3, C4 = (-205.0 / 72.0, 8.0 / 5.0, -1.0 / 5.0, 8.0 / 315.0, -1.0 / 560.0)
MESH = pl.DeviceIdType.MESH
F32 = jnp.float32
SHOTS, DOM, STEPS = 8, 16, 8
HALO = 8
PLANES, ROWS = 48, 48


def chunk_of(d):
    return d + (d // 8) * (23 - 2 * d)


def band():
    row = lax.broadcasted_iota(jnp.int32, (256, 256), 0)
    col = lax.broadcasted_iota(jnp.int32, (256, 256), 1)
    gap = jnp.abs((row & 127) - (col & 127))
    same = ((row >> 6) & 1) == ((col >> 6) & 1)
    full = jnp.where(same & (gap == 0), 3.0 * C0, 0.0)
    for k, c in ((1, C1), (2, C2), (3, C3), (4, C4)):
        full = full + jnp.where(same & (gap == k), c, 0.0)
    high = full.astype(jnp.bfloat16).astype(F32)
    low = jnp.where(row < 128, full - high, 0.0)
    return jnp.where(col < 128, high, low).astype(jnp.bfloat16)


def stencil(ref, z0, weights):
    low = lax.broadcasted_iota(jnp.int32, (8, 128), 1) < 64
    cells = jnp.concatenate([ref[z0 + p, pl.ds(8, 32), :] for p in range(8)], 0)
    high = cells.astype(jnp.bfloat16)
    rest = (cells - high.astype(F32)).astype(jnp.bfloat16)
    along_y = jnp.dot(jnp.concatenate([high, rest], 1), weights, preferred_element_type=F32)
    along_y = along_y[:, :128] + along_y[:, 128:]
    for p in range(8):
        z = z0 + p
        for i in range(4):
            row = 8 + 8 * i
            mid = ref[z, pl.ds(row, 8), :]
            pairs = [ref[z + k, pl.ds(row, 8), :] + ref[z - k, pl.ds(row, 8), :] for k in (1, 2, 3, 4)]
            up1, up2, dn1, dn2 = (ref[z, pl.ds(row + k, 8), :] for k in (1, 2, -1, -2))
            pairs[1] = pairs[1] + (up1 + dn1)
            pairs[3] = pairs[3] + (up2 + dn2)
            odd = C1 * (jnp.where(low, up1, mid) + jnp.where(low, mid, dn1))
            odd = odd + C3 * (jnp.where(low, up2, up1) + jnp.where(low, dn1, dn2))
            total = C1 * pairs[0] + C2 * pairs[1] + C3 * pairs[2] + C4 * pairs[3]
            lap = total + pltpu.roll(odd, 64, 1) + along_y[32 * p + 8 * i : 32 * p + 8 * i + 8]
            yield z, i, mid, lap


def kernel(
    vel, fwd_cur, fwd_prev, adj_cur, adj_prev, rec_pos, observed, wavelet, src_pos, count, aperture, block_slot,
    out,
    v_2a, v_2b, picks, m_b, m_t, m_1, f_in, f_t, f_1,
    u_a, u_b, p_a, p_b, p_p, w_a, w_b, m_x, laps, res, hits, onehot, weights, grad, land, land_m, land_p,
    g_1, g_send, g_t, g_b, g_recv, batch,
    in_sem, own_sem, va_s, va_r, f_s, f_r, vb_s, vb_r, vc_s, vc_r, gd_s, gd_r, gf_s, gf_r, gg_s, gg_r,
    h_s, h_r, hm_s, hm_r, hp_s, hp_r,
):
    s, d = lax.axis_index("shot"), lax.axis_index("dom")
    e = chunk_of(d)
    x, half_id = s // 2, lax.rem(s, 2)

    loads = []
    for f, ref in enumerate((fwd_cur, fwd_prev, adj_cur, adj_prev)):
        loads.append(pltpu.make_async_copy(ref, f_in.at[f], in_sem.at[f]))
        loads[-1].start()

    barrier = pltpu.get_barrier_semaphore()
    for o in range(1, DOM):
        pl.semaphore_signal(barrier, inc=1, device_id=(s, lax.rem(d + o, DOM)), device_id_type=MESH)
    for o in range(1, SHOTS):
        pl.semaphore_signal(barrier, inc=1, device_id=(lax.rem(s + o, SHOTS), d), device_id_type=MESH)

    def partner(o):
        return lax.rem(d // 8 + o // 8, 2) * 8 + lax.rem(d + o, 8)

    def over_dom(src, dst, send, recv):
        def copy(o):
            p = partner(o)
            return pltpu.make_async_remote_copy(
                src_ref=src(p), dst_ref=dst, send_sem=send(o), recv_sem=recv(o), device_id=(s, p), device_id_type=MESH
            )

        return copy, DOM

    def over_shot(src, dst, send, recv):
        def copy(o):
            p = lax.rem(s + o, SHOTS)
            return pltpu.make_async_remote_copy(
                src_ref=src(p), dst_ref=dst, send_sem=send(o), recv_sem=recv(o), device_id=(p, d), device_id_type=MESH
            )

        return copy, SHOTS

    def over_x(src, dst, send, recv):
        def copy(o):
            p = lax.rem(s + 2 * o, SHOTS)
            return pltpu.make_async_remote_copy(
                src_ref=src(p), dst_ref=dst, send_sem=send(o), recv_sem=recv(o), device_id=(p, d), device_id_type=MESH
            )

        return copy, SHOTS // 2

    def start(exchange, own):
        copy, n = exchange

        def body(k, c):
            copy(2 * k - 1 - 7 * (k // 5) if n == SHOTS else n - k).start()
            return c

        lax.fori_loop(1, n, body, 0, unroll=True)
        own.start()

    def finish(exchange, own):
        copy, n = exchange

        def body(o, c):
            copy(o).wait()
            return c

        lax.fori_loop(1, n, body, 0, unroll=True)
        own.wait()

    def transpose_pair(src, dst, xp):
        def body(q, c):
            block = src[pl.ds(2 * xp, 2), :, pl.ds(pl.multiple_of(q * 128, 128), 128)]
            dst[xp, pl.ds(q * 128, 128), :] = block.reshape(128, 128).T
            return c

        lax.fori_loop(0, 4, body, 0)

    def transpose_in(src, dst):
        for xp in range(2):
            transpose_pair(src, dst, xp)

    def z_of(p):
        return pl.ds(chunk_of(p) * 32, 32)

    def rows_of(p):
        return pl.ds(p * 8, 8)

    def quarter(p):
        return pl.ds((p // 2) * 16, 16)

    loads[0].wait()
    transpose_in(f_in.at[0], f_t.at[0])
    pl.semaphore_wait(barrier, DOM + SHOTS - 2)
    va, va_own = [], []
    for h in range(2):
        half = pl.ds(2 * h, 2)
        mine = (v_2a, v_2b)[h].at[pl.ds(2 * x, 2)]
        va.append(
            over_x(
                lambda p, half=half: vel.at[:, half, quarter(p), :],
                mine,
                lambda o, h=h: va_s.at[h, o],
                lambda o, h=h: va_r.at[h, o],
            )
        )
        va_own.append(pltpu.make_async_copy(vel.at[:, half, quarter(s), :], mine, own_sem.at[0, h]))
        start(va[h], va_own[h])

    fields, fields_own = [], []
    for f in range(4):
        fields.append(
            over_dom(
                lambda p, f=f: f_t.at[f, :, z_of(p), :],
                f_1.at[f, pl.ds(2 * d, 2)],
                lambda o, f=f: f_s.at[f, o],
                lambda o, f=f: f_r.at[f, o],
            )
        )
        fields_own.append(pltpu.make_async_copy(f_t.at[f, :, z_of(d), :], f_1.at[f, pl.ds(2 * d, 2)], own_sem.at[1 + f, 0]))
    start(fields[0], fields_own[0])
    loads[1].wait()
    transpose_in(f_in.at[1], f_t.at[1])
    start(fields[1], fields_own[1])
    for f in range(2, 4):
        loads[f].wait()
        transpose_in(f_in.at[f], f_t.at[f])

    def send_adjoint(lo, hi):
        for f in range(2, 4):

            def body(o, c, f=f):
                fields[f][0](o).start()
                return c

            lax.fori_loop(lo, hi, body, 0)

    for f in range(2, 4):
        fields_own[f].start()

    pos = rec_pos[...]
    rec_row = (((pos & 511) - 32 * e + 4) << 5) + (pos >> 16)
    rec_lane = (((pos >> 15) & 1) << 6) + ((pos >> 9) & 63)
    row_id = lax.broadcasted_iota(jnp.int32, (256, 256), 0)
    for g in range(5):
        onehot[g] = (row_id + 256 * g == rec_row).astype(F32).astype(jnp.bfloat16)
    lanes = (lax.broadcasted_iota(jnp.int32, (128, 256), 0) == rec_lane).astype(F32)

    def dot(g, b):
        found = lax.dot_general(onehot[g], b, (((1,), (1,)), ((), ())), preferred_element_type=F32)
        return found.reshape(8, 32, 128)

    ones = lanes.astype(jnp.bfloat16)
    for g in range(5):
        hits[pl.ds(8 * g, 8)] = dot(g, ones)

    def record(t, c):
        b = lanes * observed[pl.ds(t, 1), :]
        high = b.astype(jnp.bfloat16)
        low = (b - high.astype(F32)).astype(jnp.bfloat16)
        for g in range(5):
            res[t, pl.ds(8 * g, 8)] = dot(g, high) + dot(g, low)
        return c

    lax.fori_loop(0, STEPS, record, 0)

    def clear(z, c):
        for ref in (u_a, u_b, p_a, p_b, p_p, w_a, w_b, m_x):
            ref[z] = jnp.zeros((ROWS, 128), F32)
        return c

    lax.fori_loop(0, PLANES, clear, 0)
    weights[...] = band()

    def slot_of(shot, col):
        first = aperture[shot, 0]
        block_x = (first >> 3) + ((col - (first >> 3)) & 15)
        return block_slot[((block_x >> 4) << 3) + (first & 7)]

    vb, vb_own = [], []
    for h in range(2):
        finish(va[h], va_own[h])

        def pick(shot, c, h=h):
            slot = slot_of(shot, d)
            picks[h, shot] = (v_2a, v_2b)[h][((slot >> 2) << 1) + (slot & 1)]
            return c

        lax.fori_loop(0, SHOTS, pick, 0)
        offer = m_b.at[half_id, pl.ds(2 * h, 2), quarter(s), :]
        vb.append(
            over_shot(lambda p, h=h: picks.at[h, p], offer, lambda o, h=h: vb_s.at[h, o], lambda o, h=h: vb_r.at[h, o])
        )
        vb_own.append(pltpu.make_async_copy(picks.at[h, s], offer, own_sem.at[5, h]))
        start(vb[h], vb_own[h])
    send_adjoint(1, 8)

    def relayout(f, dst):
        flat = dst.reshape(PLANES * ROWS, 128)

        def body(r, c):
            for g in range(4):
                flat[pl.ds((HALO + 8 * g) * ROWS + 8 + r, 8, stride=ROWS), :] = f_1[f, r, pl.ds(8 * g, 8), :]
            return c

        lax.fori_loop(0, 32, body, 0)

    def halo(src, n, land_ref, send, recv):
        def ends():
            right = pltpu.make_async_remote_copy(
                src_ref=src.at[pl.ds(HALO + 32 - n, n), pl.ds(8, 32), :],
                dst_ref=land_ref.at[0],
                send_sem=send.at[0],
                recv_sem=recv.at[0],
                device_id=(s, chunk_of(lax.rem(e + 1, DOM))),
                device_id_type=MESH,
            )
            left = pltpu.make_async_remote_copy(
                src_ref=src.at[pl.ds(HALO, n), pl.ds(8, 32), :],
                dst_ref=land_ref.at[1],
                send_sem=send.at[1],
                recv_sem=recv.at[1],
                device_id=(s, chunk_of(lax.rem(e + DOM - 1, DOM))),
                device_id_type=MESH,
            )
            return right, left

        def begin():
            right, left = ends()
            pl.when(e < DOM - 1)(right.start)
            pl.when(e > 0)(left.start)

        def sent():
            right, left = ends()
            pl.when(e < DOM - 1)(right.wait_send)
            pl.when(e > 0)(left.wait_send)

        def arrived(use):
            right, left = ends()

            @pl.when(e > 0)
            def _():
                right.wait_recv()
                use(0, HALO - n)

            @pl.when(e < DOM - 1)
            def _():
                left.wait_recv()
                use(1, HALO + 32)

        return begin, sent, arrived

    def put(dst, land_ref, n):
        def use(side, at):
            def body(z, c):
                dst[at + z, pl.ds(8, 32), :] = land_ref[side, z]
                return c

            lax.fori_loop(0, n, body, 0)

        return use

    def u_halo(par):
        return halo(u_a, 8, land.at[par], h_s.at[par], h_r.at[par])

    finish(fields[0], fields_own[0])
    relayout(0, u_a)
    u_halo(0)[0]()
    finish(fields[1], fields_own[1])
    relayout(1, u_b)
    prev_halo = halo(u_b, 4, land_p.at[0], hp_s.at[0], hp_r.at[0])
    prev_halo[0]()

    in_first = (jnp.full((128, 128), slot_of(s, d), jnp.int32) & 2) == 0
    vc, vc_own = [], []
    for h in range(2):
        finish(vb[h], vb_own[h])

        def choose(q, c, h=h):
            cols = pl.ds(pl.multiple_of(q * 128, 128), 128)
            two = [m_b[part, pl.ds(2 * h, 2), :, cols].reshape(128, 128) for part in range(2)]
            m_t[h, pl.ds(q * 128, 128), :] = jnp.where(in_first, two[0], two[1]).T
            return c

        lax.fori_loop(0, 4, choose, 0)
        vc.append(
            over_dom(
                lambda p, h=h: m_t.at[h, z_of(p), :],
                m_1.at[d, h],
                lambda o, h=h: vc_s.at[h, o],
                lambda o, h=h: vc_r.at[h, o],
            )
        )
        vc_own.append(pltpu.make_async_copy(m_t.at[h, z_of(d), :], m_1.at[d, h], own_sem.at[6, h]))
        start(vc[h], vc_own[h])
    send_adjoint(8, 10)
    prev_halo[2](put(u_b, land_p.at[0], 4))
    prev_halo[1]()
    for h in range(2):
        finish(vc[h], vc_own[h])
    m_flat = m_x.reshape(PLANES * ROWS, 128)
    base_x = aperture[s, 0] >> 3

    def place(k, c):
        slab = m_1[(base_x + k) & 15]
        for xp in range(2):
            for g in range(4):
                m_flat[pl.ds((HALO + 8 * g) * ROWS + 8 + xp + 2 * k, 8, stride=ROWS), :] = slab[xp, 8 * g : 8 * g + 8]
        return c

    lax.fori_loop(0, 16, place, 0, unroll=4)
    model_halo = halo(m_x, 8, land_m, hm_s, hm_r)
    model_halo[0]()

    source = src_pos[0]
    src_z = (source & 511) - 32 * e + HALO
    src_cell = ((source >> 16) << 7) + (((source >> 15) & 1) << 6) + ((source >> 9) & 63)
    cell = (lax.broadcasted_iota(jnp.int32, (8, 128), 0) << 7) + lax.broadcasted_iota(jnp.int32, (8, 128), 1)
    steps = jnp.full((8, 128), count[0], jnp.int32)

    def tile(i):
        return pl.ds(8 + 8 * i, 8)

    def inner(i):
        return pl.ds(8 * i, 8)

    def blocks(body, first, stride, n):
        def one(j, c):
            body(first + stride * j)
            return c

        lax.fori_loop(0, n, one, 0)

    def forward(src, dst, t):
        def body(z0):
            active = steps > t
            found = []
            for z, i, mid, lap in stencil(src, z0, weights[...]):
                amount = jnp.where(z == src_z, wavelet[t], 0.0)
                u = 2.0 * mid - dst[z, tile(i), :] + m_x[z, tile(i), :] * lap
                u = u + jnp.where(cell + 1024 * i == src_cell, amount, 0.0)
                miss = jnp.where(active, hits[z - 4, inner(i), :] * u - res[t, z - 4, inner(i), :], 0.0)
                found.append((z, i, lap, u, miss))
            for z, i, lap, u, miss in found:
                laps[t, z - 4, inner(i), :] = lap
                dst[z, tile(i), :] = u
                res[t, z - 4, inner(i), :] = miss

        return body

    def fwd_pair(i, c):
        par, then = lax.rem(i, 2), lax.rem(i + 1, 2)
        step = forward(u_a, u_b, 2 * i)
        blocks(step, 12, 8, 3)

        @pl.when(i == 0)
        def _():
            model_halo[2](put(m_x, land_m, 8))
            model_halo[1]()

        @pl.when(i == STEPS // 2 - 1)
        def _():
            for f, dst in ((2, p_a), (3, p_p)):
                finish(fields[f], fields_own[f])
                relayout(f, dst)

        u_halo(par)[2](put(u_a, land.at[par], 8))
        blocks(step, 4, 32, 2)
        u_halo(par)[1]()
        step = forward(u_b, u_a, 2 * i + 1)
        blocks(step, 8, 24, 2)


        @pl.when(i < STEPS // 2 - 1)
        def _():
            u_halo(then)[0]()
            send_adjoint(10 + 2 * i, 12 + 2 * i)

        blocks(step, 16, 8, 2)
        return c

    lax.fori_loop(0, STEPS // 2, fwd_pair, 0)

    def p_halo(par):
        return halo(p_a, 8, land.at[par], h_s.at[par], h_r.at[par])

    def first(z, c):
        active = steps > STEPS - 1
        found = []
        for i in range(4):
            hit = p_a[z, tile(i), :] + res[STEPS - 1, z - 4, inner(i), :]
            part = jnp.where(active, hit * laps[STEPS - 1, z - 4, inner(i), :], 0.0)
            found.append((i, hit, m_x[z, tile(i), :] * hit, part))
        for i, hit, w, part in found:
            p_a[z, tile(i), :] = hit
            w_a[z, tile(i), :] = w
            grad[z - 4, inner(i), :] = part
        return c

    lax.fori_loop(8, 16, first, 0)
    lax.fori_loop(32, 40, first, 0)
    p_halo(0)[0]()
    adj_prev_halo = halo(p_p, 4, land_p.at[1], hp_s.at[1], hp_r.at[1])
    adj_prev_halo[0]()
    lax.fori_loop(16, 32, first, 0)

    def clear_ends(z, c):
        grad[z] = jnp.zeros((32, 128), F32)
        grad[36 + z] = jnp.zeros((32, 128), F32)
        return c

    lax.fori_loop(0, 4, clear_ends, 0)

    def backward(src, dst, p_now, p_then, t):
        def body(z0):
            active, then = steps > t, steps > t - 1
            found = []
            for z, i, _, lap in stencil(src, z0, weights[...]):
                hit = p_now[z, tile(i), :]
                prev = p_p[z, tile(i), :]
                cur = jnp.where(active, 2.0 * hit - prev + lap, hit)
                prev = jnp.where(active, hit, prev)
                hit = cur + res[t - 1, z - 4, inner(i), :]
                part = jnp.where(then, hit * laps[t - 1, z - 4, inner(i), :], 0.0)
                found.append((z, i, prev, hit, m_x[z, tile(i), :] * hit, grad[z - 4, inner(i), :] + part))
            for z, i, prev, hit, w, total in found:
                p_p[z, tile(i), :] = prev
                p_then[z, tile(i), :] = hit
                dst[z, tile(i), :] = w
                grad[z - 4, inner(i), :] = total

        return body

    def adj_ends(land_ref, t):
        stepped = steps > t + 1

        def use(side, at):
            near = at + 4 * (1 - side)

            def keep(z, c):
                for i in range(4):
                    p_p[z, tile(i), :] = jnp.where(stepped, p_b[z, tile(i), :], p_p[z, tile(i), :])
                return c

            lax.fori_loop(near, near + 4, keep, 0)

            def body(z, c):
                hit = land_ref[side, z]
                p_a[at + z, pl.ds(8, 32), :] = hit
                w_a[at + z, pl.ds(8, 32), :] = m_x[at + z, pl.ds(8, 32), :] * hit
                return c

            lax.fori_loop(0, 8, body, 0)

        return use

    def adj_pair(i, c):
        par, then = lax.rem(i, 2), lax.rem(i + 1, 2)
        t = STEPS - 1 - 2 * i
        step = backward(w_a, w_b, p_a, p_b, t)
        pl.when(i == 0)(adj_prev_halo[1])
        blocks(step, 12, 8, 3)

        @pl.when(i == 0)
        def _():
            adj_prev_halo[2](put(p_p, land_p.at[1], 4))

        p_halo(par)[2](adj_ends(land.at[par], t))
        blocks(step, 4, 32, 2)
        p_halo(par)[1]()

        @pl.when(i < STEPS // 2 - 1)
        def _():
            step = backward(w_b, w_a, p_b, p_a, t - 1)
            blocks(step, 8, 24, 2)
            p_halo(then)[0]()
            blocks(step, 16, 8, 2)

        return c

    lax.fori_loop(0, STEPS // 2, adj_pair, 0)

    g_flat = grad.reshape(40 * 32, 128)

    gd, gd_own = [], []
    for h in range(2):

        def gather(k, c, h=h):
            for g in range(4):
                g_1[h, k, pl.ds(8 * g, 8), :] = g_flat[pl.ds((4 + 8 * g) * 32 + h + 2 * k, 8, stride=32), :]
            return c

        lax.fori_loop(0, 16, gather, 0, unroll=4)

        def turn(col, c, h=h):
            g_send[h, col] = g_1[h, (col - base_x) & 15]
            return c

        lax.fori_loop(0, 16, turn, 0, unroll=4)
        gd.append(
            over_dom(
                lambda p, h=h: g_send.at[h, p],
                g_t.at[h, z_of(d), :],
                lambda o, h=h: gd_s.at[h, o],
                lambda o, h=h: gd_r.at[h, o],
            )
        )
        gd_own.append(pltpu.make_async_copy(g_send.at[h, d], g_t.at[h, z_of(d), :], own_sem.at[7, h]))
        start(gd[h], gd_own[h])

    gf, gf_own = [], []
    for h in range(2):
        finish(gd[h], gd_own[h])
        half = pl.ds(2 * h, 2)

        def back(q, c, h=h, half=half):
            cols = pl.ds(pl.multiple_of(q * 128, 128), 128)
            g_b[half, :, cols] = g_t[h, pl.ds(q * 128, 128), :].T.reshape(2, 64, 128)
            return c

        lax.fori_loop(0, 4, back, 0)
        gf.append(
            over_shot(
                lambda p, half=half: g_b.at[half, rows_of(p), :],
                g_recv.at[h, s],
                lambda o, h=h: gf_s.at[h, o],
                lambda o, h=h: gf_r.at[h, o],
            )
        )
        gf_own.append(pltpu.make_async_copy(g_b.at[half, rows_of(s), :], g_recv.at[h, s], own_sem.at[8, h]))
        start(gf[h], gf_own[h])

    owners = [jnp.full((8, 128), slot_of(shot, d), jnp.int32) for shot in range(SHOTS)]
    gg, gg_own = [], []
    for h in range(2):
        finish(gf[h], gf_own[h])
        half = pl.ds(2 * h, 2)

        def add_up(slot, c, h=h):
            mine = [owner == slot for owner in owners]
            sums = []
            for x in range(2):
                for q in range(4):
                    total = jnp.zeros((8, 128), F32)
                    for shot in range(SHOTS):
                        total = total + jnp.where(mine[shot], g_recv[h, shot, x, :, pl.ds(128 * q, 128)], 0.0)
                    sums.append((x, q, total))
            for x, q, total in sums:
                batch[h, slot, x, :, pl.ds(128 * q, 128)] = total
            return c

        lax.fori_loop(0, 16, add_up, 0)
        target = out.at[:, half, rows_of(s), :]
        gg.append(
            over_shot(
                lambda p, h=h: batch.at[h, pl.ds(2 * p, 2)],
                target,
                lambda o, h=h: gg_s.at[h, o],
                lambda o, h=h: gg_r.at[h, o],
            )
        )
        gg_own.append(pltpu.make_async_copy(batch.at[h, pl.ds(2 * s, 2)], target, own_sem.at[9, h]))
        start(gg[h], gg_own[h])
    for h in range(2):
        finish(gg[h], gg_own[h])


def local(
    velocity,
    fwd_prev,
    fwd_cur,
    adj_prev,
    adj_cur,
    wavelet,
    src_pos,
    rec_pos,
    observed,
    step_count,
    aperture,
    block_slot,
    prev_batch,
    snapshot,
):
    shape = (2, 4, 64, 512)
    hbm = pl.BlockSpec(memory_space=pl.ANY)
    vmem = pl.BlockSpec(memory_space=pltpu.VMEM)
    smem = pl.BlockSpec(memory_space=pltpu.SMEM)
    field = pltpu.VMEM((PLANES, ROWS, 128), F32)
    dma = pltpu.SemaphoreType.DMA
    scratch = [
        pltpu.VMEM((8, 2, 16, 512), F32),
        pltpu.VMEM((8, 2, 16, 512), F32),
        pltpu.VMEM((2, 8, 2, 16, 512), F32),
        pltpu.VMEM((2, 4, 64, 512), F32),
        pltpu.VMEM((2, 512, 128), F32),
        pltpu.VMEM((16, 2, 32, 128), F32),
        pltpu.VMEM((4, 4, 64, 512), F32),
        pltpu.VMEM((4, 2, 512, 128), F32),
        pltpu.VMEM((4, 32, 32, 128), F32),
        *[field] * 8,
        pltpu.VMEM((STEPS, 40, 32, 128), F32),
        pltpu.VMEM((STEPS, 40, 32, 128), F32),
        pltpu.VMEM((40, 32, 128), F32),
        pltpu.VMEM((5, 256, 256), jnp.bfloat16),
        pltpu.VMEM((256, 256), jnp.bfloat16),
        pltpu.VMEM((40, 32, 128), F32),
        pltpu.VMEM((2, 2, 8, 32, 128), F32),
        pltpu.VMEM((2, 8, 32, 128), F32),
        pltpu.VMEM((2, 2, 4, 32, 128), F32),
        pltpu.VMEM((2, 16, 32, 128), F32),
        pltpu.VMEM((2, 16, 32, 128), F32),
        pltpu.VMEM((2, 512, 128), F32),
        pltpu.VMEM((4, 64, 512), F32),
        pltpu.VMEM((2, 8, 2, 8, 512), F32),
        pltpu.VMEM((2, 16, 2, 8, 512), F32),
        dma((4,)),
        dma((10, 2)),
        dma((2, 4)), dma((2, 4)),
        dma((4, 16)), dma((4, 16)),
        dma((2, 8)), dma((2, 8)),
        dma((2, 16)), dma((2, 16)),
        dma((2, 16)), dma((2, 16)),
        dma((2, 8)), dma((2, 8)),
        dma((2, 8)), dma((2, 8)),
        dma((2, 2)), dma((2, 2)),
        dma((2,)), dma((2,)),
        dma((2, 2)), dma((2, 2)),
    ]
    batch = pl.pallas_call(
        kernel,
        out_shape=jax.ShapeDtypeStruct(shape, F32),
        in_specs=[hbm] * 5 + [vmem] * 2 + [smem] * 5,
        out_specs=hbm,
        scratch_shapes=scratch,
        name="adjoint_gradient",
        compiler_params=pltpu.CompilerParams(collective_id=0, has_side_effects=True, vmem_limit_bytes=56 << 20),
    )(
        velocity.reshape(shape),
        fwd_cur[0],
        fwd_prev[0],
        adj_cur[0],
        adj_prev[0],
        rec_pos,
        observed[0],
        wavelet[0],
        src_pos,
        step_count,
        aperture,
        block_slot,
    )
    result = (batch - prev_batch.reshape(shape)) + snapshot.reshape(shape)
    return result.reshape(velocity.shape)


def solution(mesh):
    placed = (
        P("shot", "dom", None, None, None),
        P("shot", "dom", None, None),
        P("shot", "dom", None, None),
        P("shot", "dom", None, None),
        P("shot", "dom", None, None),
        P("shot", None),
        P("shot"),
        P("shot", None),
        P("shot", None, None),
        P("shot"),
        P(),
        P(),
        P("shot", "dom", None, None, None),
        P("shot", "dom", None, None, None),
    )
    return jax.shard_map(
        local,
        mesh=mesh,
        in_specs=placed,
        out_specs=P("shot", "dom", None, None, None),
        check_vma=False,
    )
```
